32 devices in a mesh: seq: 8 (over z, x), head: 4 (over y, core).
Axes of the slice: x: 2, y: 2, z: 4, core: 2. Of those that a mesh axis runs over, the one named last changes fastest.
Arguments:
- queries: bfloat16 [4096, 4096], P('seq', 'head'), may hold values from -6 to 6
- keys: bfloat16 [4096, 1024], P('seq', 'head'), may hold values from -6 to 6
- values: bfloat16 [4096, 1024], P('seq', 'head'), may hold values from -6 to 6
- output_gradient: bfloat16 [4096, 4096], P('seq', 'head'), may hold values from -6 to 6
- doc_lengths: int32 [32], P(('seq', 'head')), may hold values from 1 to 512, 4096 in all
Outputs:
- grad_queries: bfloat16 [4096, 4096], P('seq', 'head')
- key_gradient: bfloat16 [4096, 1024], P('seq', 'head')
- value_gradient: bfloat16 [4096, 1024], P('seq', 'head')
The draws below stay inside these ranges and needn't reach their ends.
Inputs may be any that keep to these rules, and one draw needn't show every extreme that they name: `doc_lengths`: the lengths sum to 4096; no document holds more than 512 tokens, and one holds exactly 512.
All inputs are finite; a program needn't handle non-finite values. No bound on the sum of `doc_lengths` on one device may be relied on, other than what follows from the above.
Results may differ from the reference program's by a relative error of at most 0.012.
Values may be sent and summed in bfloat16 or wider, within the bound.
No kernel may reach another device: no remote copies, remote signals or barrier semaphores. Data moves between devices by JAX's collectives and lax.ppermute only.
A program may use at most 64 MiB of HBM per device.

```python
import math
import jax
import jax.numpy as jnp
import numpy as np
from jax import lax

QUERY_HEADS = 32
KEY_VALUE_HEADS = 8
HEAD_WIDTH = 128
TOKENS_PER_SHARD = 512
SEQUENCE_TOKENS = 4096
DOCS = 32


def draw_keys(key, part):
    key = jax.random.fold_in(key, 11)
    final_result = jnp.clip(jax.random.normal(key, (SEQUENCE_TOKENS, KEY_VALUE_HEADS * HEAD_WIDTH), jnp.float32), -6.0, 6.0)
    return final_result.astype(jnp.bfloat16)


def draw_queries(key, part):
    key = jax.random.fold_in(key, 23)
    final_result = jnp.clip(jax.random.normal(key, (SEQUENCE_TOKENS, QUERY_HEADS * HEAD_WIDTH), jnp.float32), -6.0, 6.0)
    return final_result.astype(jnp.bfloat16)


def block_levels(stream_key, extent, shards, low, top_value):
    gain = 1.0
    for axis_at, parts in shards:
        draws = jax.random.uniform(jax.random.fold_in(jax.random.fold_in(stream_key, 6), axis_at), (parts,), jnp.float32, low / len(shards), top_value / len(shards))
        gain = gain * jnp.repeat(jnp.exp(draws), extent[axis_at] // parts).reshape((-1,) + (1,) * (len(extent) - 1 - axis_at))
    return gain


def length_profile(amount, total, bound, skew):
    portions = [(1 << 20) // math.isqrt(rank ** skew) + 1 for rank in range(2, amount + 1)]
    spare, holding = total - bound - (amount - 1), [1] * (amount - 1)
    while spare > 0:
        candidates = [i for i in range(amount - 1) if holding[i] < bound]
        whole, left = sum([portions[i] for i in candidates]), spare
        for i in candidates:
            addition = min(bound - holding[i], max(1, left * portions[i] // whole), spare)
            holding[i] = holding[i] + addition
            spare = spare - addition
    return np.array([bound] + holding)


def ragged(own_key, count, total, reach, lean):
    if count == 2:
        one = jax.random.randint(own_key, (), max(1, total - reach), min(reach, total - 1) + 1)
        return jnp.stack([one, total - one])
    sizes = jnp.asarray(length_profile(count, total, reach, lean), jnp.int32)
    couples = (count - 1) // 2
    giver, sink = sizes[1:1 + 2 * couples:2], sizes[2:2 + 2 * couples:2]
    slack = jnp.minimum(giver - 1, reach - sink)
    moved = jax.random.randint(jax.random.fold_in(own_key, 1), (couples,), 0, 1 << 20) % (slack + 1)
    sizes = sizes.at[1:1 + 2 * couples:2].set(giver - moved).at[2:2 + 2 * couples:2].set(sink + moved)
    return sizes[jax.random.permutation(jax.random.fold_in(own_key, 2), count)]


def gaussian(stream_key, shape, deviation, limit, shards=(), kind=jnp.bfloat16):
    values = deviation * jax.random.normal(stream_key, shape, jnp.float32)
    if shards:
        values = values * block_levels(stream_key, shape, shards, -0.22, 0.18)
    return jnp.clip(values, -limit, limit).astype(kind)


def setup_inputs(seed: int = 0) -> dict:
    seeds = jax.random.split(jax.random.key(seed), 6)
    queries = draw_queries(jax.random.fold_in(seeds[5], 71), 0)
    keys = draw_keys(jax.random.fold_in(seeds[5], 71), 0)
    values = gaussian(seeds[2], (SEQUENCE_TOKENS, KEY_VALUE_HEADS * HEAD_WIDTH), 1.0, 6.0, ((0, 8), (1, 4)))
    output_gradient = gaussian(seeds[3], (SEQUENCE_TOKENS, QUERY_HEADS * HEAD_WIDTH), 1.0, 6.0, ((0, 8), (1, 4)))
    doc_lengths = ragged(seeds[4], DOCS, SEQUENCE_TOKENS, TOKENS_PER_SHARD, 2).astype(jnp.int32)
    return dict(queries=queries, keys=keys, values=values, output_gradient=output_gradient, doc_lengths=doc_lengths)


def doc_starts(lengths, positions):
    ends = jnp.cumsum(lengths, dtype=jnp.int32)
    starts = (ends - lengths).astype(jnp.int32)
    reached = starts[None, :] <= positions[:, None]
    return jnp.max(jnp.where(reached, starts[None, :], jnp.int32(0)), axis=1).astype(jnp.int32)


def reference(queries, keys, values, output_gradient, doc_lengths):
    row_total_count = queries.shape[0]
    block_list = row_total_count // TOKENS_PER_SHARD
    heads_per_group = QUERY_HEADS // KEY_VALUE_HEADS
    scale = HEAD_WIDTH ** -0.5
    positions = jnp.arange(row_total_count, dtype=jnp.int32)
    starts = doc_starts(doc_lengths, positions)
    query_five_axes = queries.reshape(block_list, TOKENS_PER_SHARD, KEY_VALUE_HEADS, heads_per_group, HEAD_WIDTH)
    gradient_five_axes = output_gradient.reshape(block_list, TOKENS_PER_SHARD, KEY_VALUE_HEADS, heads_per_group, HEAD_WIDTH)
    key_four_axes = keys.reshape(block_list, TOKENS_PER_SHARD, KEY_VALUE_HEADS, HEAD_WIDTH)
    value_four_axes = values.reshape(block_list, TOKENS_PER_SHARD, KEY_VALUE_HEADS, HEAD_WIDTH)
    key_prev = jnp.concatenate([jnp.zeros_like(key_four_axes[:1]), key_four_axes[:-1]], axis=0)
    value_prev = jnp.concatenate([jnp.zeros_like(value_four_axes[:1]), value_four_axes[:-1]], axis=0)
    pos_rows = positions.reshape(block_list, TOKENS_PER_SHARD)
    start_rows = starts.reshape(block_list, TOKENS_PER_SHARD)

    def window(args):
        query_block, grad_block, kp, vp, ko, vo, query_pos, query_start = args
        key_rows = jnp.concatenate([kp, ko], axis=0).astype(jnp.float32)
        value_rows = jnp.concatenate([vp, vo], axis=0).astype(jnp.float32)
        key_pos = jnp.concatenate([query_pos - TOKENS_PER_SHARD, query_pos]).astype(jnp.int32)
        allowed = (key_pos[None, :] >= query_start[:, None]) & (key_pos[None, :] <= query_pos[:, None])
        query_f = query_block.astype(jnp.float32)
        grad_f = grad_block.astype(jnp.float32)
        raw = jnp.einsum("qgha,kga->ghqk", query_f, key_rows)
        scores = jnp.where(allowed[None, None], raw * scale, -jnp.inf)
        expo = jnp.exp(scores - jnp.max(scores, axis=-1, keepdims=True))
        prob = expo / jnp.sum(expo, axis=-1, keepdims=True)
        weights = lax.optimization_barrier(prob.astype(jnp.bfloat16)).astype(jnp.float32)
        out = jnp.einsum("ghqk,kga->qgha", weights, value_rows)
        delta = jnp.sum(grad_f * out, axis=-1)
        dprob = jnp.einsum("qgha,kga->ghqk", grad_f, value_rows)
        dscore = (prob * (dprob - jnp.transpose(delta, (1, 2, 0))[..., None]) * scale).astype(jnp.bfloat16)
        dscore = lax.optimization_barrier(dscore).astype(jnp.float32)
        grad_q = jnp.einsum("ghqk,kga->qgha", dscore, key_rows)
        grad_k = jnp.einsum("ghqk,qgha->kga", dscore, query_f)
        grad_v = jnp.einsum("ghqk,qgha->kga", weights, grad_f)
        return (grad_q.astype(jnp.bfloat16), grad_k[:TOKENS_PER_SHARD], grad_k[TOKENS_PER_SHARD:], grad_v[:TOKENS_PER_SHARD], grad_v[TOKENS_PER_SHARD:])

    grad_q, dk_prev, dk_own, dv_prev, dv_own = lax.map(
        window, (query_five_axes, gradient_five_axes, key_prev, value_prev, key_four_axes, value_four_axes, pos_rows, start_rows))
    padding = jnp.zeros_like(dk_prev[:1])
    key_gradient = (dk_own + jnp.concatenate([dk_prev[1:], padding], axis=0)).astype(jnp.bfloat16)
    value_gradient = (dv_own + jnp.concatenate([dv_prev[1:], padding], axis=0)).astype(jnp.bfloat16)
    return (grad_q.reshape(row_total_count, QUERY_HEADS * HEAD_WIDTH),
            key_gradient.reshape(row_total_count, KEY_VALUE_HEADS * HEAD_WIDTH),
            value_gradient.reshape(row_total_count, KEY_VALUE_HEADS * HEAD_WIDTH))
```

```python
import functools

import jax
import jax.numpy as jnp
from jax import lax
from jax.experimental import pallas as pl
from jax.experimental.pallas import tpu as pltpu
from jax.sharding import PartitionSpec as P

HEAD_WIDTH = 128
BLOCK = 128
SCALE = HEAD_WIDTH ** (-0.5)
LOG2E = 1.4426950408889634
NT = (((1,), (1,)), ((), ()))
NN = (((1,), (0,)), ((), ()))
TN = (((0,), (0,)), ((), ()))


def dot(a, b, dims):
    return lax.dot_general(a, b, dims, preferred_element_type=jnp.float32)


def shifted(value, axis, steps):
    count = lax.axis_size(axis)
    first, last = (max(0, -steps), min(count, count - steps))
    return lax.ppermute(value, axis, [(source, source + steps) for source in range(first, last)])


def summed_everywhere(value, axes):
    for axis in axes:
        count = lax.axis_size(axis)
        if count & (count - 1):
            value = lax.psum(value, axis)
            continue
        step = 1
        while step < count:
            value = value + lax.ppermute(value, axis, [(s, s ^ step) for s in range(count)])
            step *= 2
    return value


def gathered_lengths(doc_lengths):
    own = doc_lengths.shape[0]
    place = lax.axis_index("seq") * lax.axis_size("head") + lax.axis_index("head")
    docs = own * lax.axis_size("seq") * lax.axis_size("head")
    row = jnp.zeros((1, docs), jnp.int32)
    row = lax.dynamic_update_slice(row, doc_lengths.reshape(1, own), (0, place * own))
    return summed_everywhere(row, ("head", "seq"))


def start_row(lengths, first, rows):
    docs = lengths.shape[1]
    before = lax.broadcasted_iota(jnp.int32, (docs, docs), 1) < lax.broadcasted_iota(
        jnp.int32, (docs, docs), 0
    )
    starts = jnp.sum(
        jnp.where(before, jnp.broadcast_to(lengths, (docs, docs)), 0), axis=1, keepdims=True
    )
    starts = jnp.broadcast_to(starts - first, (docs, rows))
    own = lax.broadcasted_iota(jnp.int32, (docs, rows), 1)
    return jnp.max(jnp.where(starts <= own, starts, -first), axis=0, keepdims=True)


def heads_stacked(ref, rows, heads):
    return jnp.concatenate(
        [ref[rows, h * HEAD_WIDTH : (h + 1) * HEAD_WIDTH] for h in range(heads)], axis=0
    )


def masked(scores, start, query, first_key, diagonal):
    keys = scores.shape[0]
    key = first_key + lax.broadcasted_iota(jnp.int32, (keys, BLOCK), 0)
    allowed = key >= start
    if diagonal:
        allowed = allowed & (key <= query)
    return jnp.concatenate(
        [
            jnp.where(allowed, scores[:, c : c + BLOCK], -jnp.inf)
            for c in range(0, scores.shape[1], BLOCK)
        ],
        axis=1,
    )


def block_scores(i, rows, heads, q_ref, k_ref, pk_ref, start):
    at = slice(i * BLOCK, (i + 1) * BLOCK)
    query_rows = heads_stacked(q_ref, at, heads)
    query = i * BLOCK + lax.broadcasted_iota(jnp.int32, (1, BLOCK), 1)
    start = start[:, at]
    prev = masked(dot(pk_ref[i * BLOCK :, :], query_rows, NT), start, query, i * BLOCK - rows, False)
    own = masked(dot(k_ref[: (i + 1) * BLOCK, :], query_rows, NT), start, query, 0, True)
    return query_rows, prev, own


def prev_kernel(
    first_ref, len_ref, q_ref, g_ref, k_ref, v_ref, pk_ref, pv_ref,
    send_ref, stat_ref, start_ref, dk_ref, dv_ref,
):
    rows, width = q_ref.shape
    heads = width // HEAD_WIDTH
    first = first_ref[0]
    start = start_row(len_ref[...], first, rows)
    start_ref[...] = start
    for i in range(rows // BLOCK):
        at = slice(i * BLOCK, (i + 1) * BLOCK)
        query_rows, prev, own = block_scores(i, rows, heads, q_ref, k_ref, pk_ref, start)
        grad_rows = heads_stacked(g_ref, at, heads)
        top = jnp.maximum(
            jnp.max(prev, axis=0, keepdims=True), jnp.max(own, axis=0, keepdims=True)
        )
        prev = jnp.exp2((prev - top) * (SCALE * LOG2E))
        own = jnp.exp2((own - top) * (SCALE * LOG2E))
        total = jnp.sum(prev, axis=0, keepdims=True) + jnp.sum(own, axis=0, keepdims=True)
        inverse = 1.0 / total
        dprev = dot(pv_ref[i * BLOCK :, :], grad_rows, NT)
        down = dot(v_ref[: (i + 1) * BLOCK, :], grad_rows, NT)
        delta = inverse * (
            jnp.sum(prev * dprev, axis=0, keepdims=True) + jnp.sum(own * down, axis=0, keepdims=True)
        )
        prob = prev * inverse
        dscore = (prob * (dprev - delta)).astype(jnp.bfloat16)
        dv = dot(prob.astype(jnp.bfloat16), grad_rows, NN)
        dk = dot(dscore, query_rows, NN)
        if i == 0:
            dv_ref[...] = dv
            dk_ref[...] = dk
        else:
            dv_ref[i * BLOCK :, :] += dv
            dk_ref[i * BLOCK :, :] += dk
        stat_ref[i, 0:1, :] = top
        stat_ref[i, 1:2, :] = inverse
        stat_ref[i, 2:3, :] = delta
    send_ref[:, :HEAD_WIDTH] = (dk_ref[...] * SCALE).astype(jnp.bfloat16)
    send_ref[:, HEAD_WIDTH:] = dv_ref[...].astype(jnp.bfloat16)


def own_kernel(
    q_ref, g_ref, k_ref, v_ref, pk_ref, pv_ref, stat_ref, start_ref,
    dq_ref, keep_ref, dk_ref, dv_ref,
):
    rows, width = q_ref.shape
    heads = width // HEAD_WIDTH
    start = start_ref[...]
    for i in reversed(range(rows // BLOCK)):
        at = slice(i * BLOCK, (i + 1) * BLOCK)
        query_rows, prev, own = block_scores(i, rows, heads, q_ref, k_ref, pk_ref, start)
        grad_rows = heads_stacked(g_ref, at, heads)
        top, inverse, delta = (stat_ref[i, n : n + 1, :] for n in range(3))
        prev = jnp.exp2((prev - top) * (SCALE * LOG2E)) * inverse
        own = jnp.exp2((own - top) * (SCALE * LOG2E)) * inverse
        dprev = dot(pv_ref[i * BLOCK :, :], grad_rows, NT)
        down = dot(v_ref[: (i + 1) * BLOCK, :], grad_rows, NT)
        dprev = (prev * (dprev - delta)).astype(jnp.bfloat16)
        down = (own * (down - delta)).astype(jnp.bfloat16)
        dv = dot(own.astype(jnp.bfloat16), grad_rows, NN)
        dk = dot(down, query_rows, NN)
        if i == rows // BLOCK - 1:
            dv_ref[...] = dv
            dk_ref[...] = dk
        else:
            dv_ref[: (i + 1) * BLOCK, :] += dv
            dk_ref[: (i + 1) * BLOCK, :] += dk
        dq = dot(pk_ref[i * BLOCK :, :], dprev, TN) + dot(k_ref[: (i + 1) * BLOCK, :], down, TN)
        for h in range(heads):
            dq_ref[at, h * HEAD_WIDTH : (h + 1) * HEAD_WIDTH] = (
                jnp.transpose(dq[:, h * BLOCK : (h + 1) * BLOCK]) * SCALE
            ).astype(jnp.bfloat16)
    keep_ref[:, :HEAD_WIDTH] = dk_ref[...] * SCALE
    keep_ref[:, HEAD_WIDTH:] = dv_ref[...]


def sum_kernel(kv_heads, *refs):
    keep, back = refs[:kv_heads], refs[kv_heads : 2 * kv_heads]
    dk_ref, dv_ref = refs[2 * kv_heads :]
    for h in range(kv_heads):
        at = slice(h * HEAD_WIDTH, (h + 1) * HEAD_WIDTH)
        total = keep[h][...] + back[h][...].astype(jnp.float32)
        dk_ref[:, at] = total[:, :HEAD_WIDTH].astype(jnp.bfloat16)
        dv_ref[:, at] = total[:, HEAD_WIDTH:].astype(jnp.bfloat16)


def column(shape, g):
    return pl.BlockSpec(shape, lambda n: (0, g))


def whole(shape):
    return pl.BlockSpec(shape, lambda n: (0,) * len(shape))


def body(queries, keys, values, output_gradient, doc_lengths):
    rows = queries.shape[0]
    kv_heads = keys.shape[1] // HEAD_WIDTH
    heads = queries.shape[1] // keys.shape[1]
    width = heads * HEAD_WIDTH
    blocks = rows // BLOCK
    prev_keys = shifted(keys, "seq", 1)
    prev_values = shifted(values, "seq", 1)
    lengths = gathered_lengths(doc_lengths)
    first = (lax.axis_index("seq") * rows).astype(jnp.int32).reshape(1)
    params = pltpu.CompilerParams(vmem_limit_bytes=48 * 1024 * 1024)
    pair = (rows, 2 * HEAD_WIDTH)
    stat = (blocks, 8, heads * BLOCK)
    operands = (queries, output_gradient, keys, values, prev_keys, prev_values)
    scratch = [pltpu.VMEM((rows, HEAD_WIDTH), jnp.float32)] * 2

    def columns(g):
        return [column((rows, width), g)] * 2 + [column((rows, HEAD_WIDTH), g)] * 4

    sends, stats = [], []
    for g in range(kv_heads):
        send, *stat_g = pl.pallas_call(
            prev_kernel,
            grid=(1,),
            out_shape=(
                jax.ShapeDtypeStruct(pair, jnp.bfloat16),
                jax.ShapeDtypeStruct(stat, jnp.float32),
                jax.ShapeDtypeStruct((1, rows), jnp.int32),
            ),
            in_specs=[pl.BlockSpec(memory_space=pltpu.SMEM), whole(lengths.shape)] + columns(g),
            out_specs=(whole(pair), whole(stat), whole((1, rows))),
            scratch_shapes=scratch,
            compiler_params=params,
            name="prev_grads",
        )(first, lengths, *operands)
        sends.append(send)
        stats.append(stat_g)
    backs = [shifted(send, "seq", -1) for send in sends]
    grads, keeps = [], []
    for g in range(kv_heads):
        aliases = {} if g == 0 else {8: 0}

        def own_call(*refs, g=g):
            return own_kernel(*(refs if g == 0 else refs[:8] + refs[9:]))

        dq, keep = pl.pallas_call(
            own_call,
            grid=(1,),
            out_shape=(
                jax.ShapeDtypeStruct(queries.shape, jnp.bfloat16),
                jax.ShapeDtypeStruct(pair, jnp.float32),
            ),
            in_specs=columns(g)
            + [whole(stat), whole((1, rows))]
            + ([] if g == 0 else [pl.BlockSpec(memory_space=pl.ANY)]),
            out_specs=(column((rows, width), g), whole(pair)),
            scratch_shapes=scratch,
            input_output_aliases=aliases,
            compiler_params=params,
            name="own_grads",
        )(*operands, *stats[g], *([] if g == 0 else [grads[-1]]))
        grads.append(dq)
        keeps.append(keep)
    key_gradient, value_gradient = pl.pallas_call(
        functools.partial(sum_kernel, kv_heads),
        out_shape=(
            jax.ShapeDtypeStruct(keys.shape, jnp.bfloat16),
            jax.ShapeDtypeStruct(values.shape, jnp.bfloat16),
        ),
        compiler_params=params,
        name="sums",
    )(*keeps, *backs)
    return (grads[-1], key_gradient, value_gradient)


def solution(mesh):
    in_specs = (
        P("seq", "head"),
        P("seq", "head"),
        P("seq", "head"),
        P("seq", "head"),
        P(("seq", "head")),
    )
    out_specs = (P("seq", "head"), P("seq", "head"), P("seq", "head"))
    return jax.shard_map(body, mesh=mesh, in_specs=in_specs, out_specs=out_specs, check_vma=False)
```

```python
import functools

import jax
import jax.numpy as jnp
from jax import lax
from jax.experimental import pallas as pl
from jax.experimental.pallas import tpu as pltpu
from jax.sharding import PartitionSpec as P

HEAD_WIDTH = 128
BLOCK = 128
SCALE = HEAD_WIDTH ** (-0.5)
LOG2E = 1.4426950408889634
NT = (((1,), (1,)), ((), ()))
NN = (((1,), (0,)), ((), ()))
TN = (((0,), (0,)), ((), ()))


def dot(a, b, dims):
    return lax.dot_general(a, b, dims, preferred_element_type=jnp.float32)


def rotated(value, axis, steps):
    count = lax.axis_size(axis)
    return lax.ppermute(value, axis, [(s, (s + steps) % count) for s in range(count)])


def summed_everywhere(value, axis, lone):
    count = lax.axis_size(axis)
    if count & (count - 1):
        return lax.psum(value, axis)
    step = 1
    while step < count:
        bits = 1 if lone or 2 * step == count else 2
        lone = False
        masks = [m * step for m in range(1, 1 << bits)]
        others = [lax.ppermute(value, axis, [(s, s ^ m) for s in range(count)]) for m in masks]
        value = functools.reduce(jnp.add, others, value)
        step <<= bits
    return value


def gathered_lengths(doc_lengths):
    own = doc_lengths.shape[0]
    shards = lax.axis_size("seq") * lax.axis_size("head")
    place = lax.axis_index("seq") * lax.axis_size("head") + lax.axis_index("head")
    spot = lax.broadcasted_iota(jnp.int32, (1, shards, own), 1) == place
    row = jnp.where(spot, doc_lengths[None, None, :], 0).reshape(1, shards * own)
    return summed_everywhere(summed_everywhere(row, "seq", True), "head", False)


def start_row(lengths, first, rows):
    docs = lengths.shape[1]
    before = lax.broadcasted_iota(jnp.int32, (docs, docs), 1) < lax.broadcasted_iota(
        jnp.int32, (docs, docs), 0
    )
    starts = jnp.sum(
        jnp.where(before, jnp.broadcast_to(lengths, (docs, docs)), 0), axis=1, keepdims=True
    )
    starts = jnp.broadcast_to(starts - first, (docs, rows))
    own = lax.broadcasted_iota(jnp.int32, (docs, rows), 1)
    return jnp.max(jnp.where(starts <= own, starts, -first), axis=0, keepdims=True)


def stacked(ref, i, g, heads):
    return jnp.concatenate(
        [
            ref[pl.ds(i * BLOCK, BLOCK), pl.ds((g * heads + h) * HEAD_WIDTH, HEAD_WIDTH)]
            for h in range(heads)
        ],
        axis=0,
    )


def masked(scores, start, query, first_key, diagonal):
    key = first_key + lax.broadcasted_iota(jnp.int32, (scores.shape[0], BLOCK), 0)
    allowed = key >= start
    if diagonal:
        allowed = allowed & (key <= query)
    return jnp.concatenate(
        [
            jnp.where(allowed, scores[:, c : c + BLOCK], -jnp.inf)
            for c in range(0, scores.shape[1], BLOCK)
        ],
        axis=1,
    )


def own_span(i):
    return slice(i * (i + 1) // 2 * BLOCK, (i + 1) * (i + 2) // 2 * BLOCK)


def prev_span(i, blocks):
    first = i * blocks - i * (i - 1) // 2
    return slice(first * BLOCK, (first + blocks - i) * BLOCK)


def query_row(i):
    return i * BLOCK + lax.broadcasted_iota(jnp.int32, (1, BLOCK), 1)


def column(g):
    return slice(g * HEAD_WIDTH, (g + 1) * HEAD_WIDTH)


def raw_kernel(q_ref, g_ref, k_ref, v_ref, *outs):
    rows, width = q_ref.shape
    kv_heads = k_ref.shape[1] // HEAD_WIDTH
    heads = width // k_ref.shape[1]
    for g in range(kv_heads):
        s_ref, d_ref = outs[2 * g : 2 * g + 2]
        for i in range(rows // BLOCK):
            seen = slice(0, (i + 1) * BLOCK)
            s_ref[own_span(i), :] = dot(k_ref[seen, column(g)], stacked(q_ref, i, g, heads), NT)
            d_ref[own_span(i), :] = dot(v_ref[seen, column(g)], stacked(g_ref, i, g, heads), NT)


def prev_kernel(
    g, first_ref, len_ref, q_ref, g_ref, pk_ref, pv_ref, s_ref, d_ref,
    send_ref, stat_ref, start_ref, ds_ref, dk_ref, dv_ref,
):
    rows, width = q_ref.shape
    heads = width // pk_ref.shape[1]
    blocks = rows // BLOCK
    start_ref[...] = start_row(len_ref[...], first_ref[0], rows)
    for i in range(blocks):
        start = start_ref[:, i * BLOCK : (i + 1) * BLOCK]
        query_rows = stacked(q_ref, i, g, heads)
        grad_rows = stacked(g_ref, i, g, heads)
        seen = slice(i * BLOCK, rows)
        prev = dot(pk_ref[seen, column(g)], query_rows, NT)
        prev = masked(prev, start, query_row(i), i * BLOCK - rows, False)
        own = masked(s_ref[own_span(i), :], start, query_row(i), 0, True)
        top = jnp.maximum(
            jnp.max(prev, axis=0, keepdims=True), jnp.max(own, axis=0, keepdims=True)
        )
        prev = jnp.exp2((prev - top) * (SCALE * LOG2E))
        own = jnp.exp2((own - top) * (SCALE * LOG2E))
        total = jnp.sum(prev, axis=0, keepdims=True) + jnp.sum(own, axis=0, keepdims=True)
        inverse = 1.0 / total
        dprev = dot(pv_ref[seen, column(g)], grad_rows, NT)
        delta = inverse * (
            jnp.sum(prev * dprev, axis=0, keepdims=True)
            + jnp.sum(own * d_ref[own_span(i), :], axis=0, keepdims=True)
        )
        prob = prev * inverse
        dscore = (prob * (dprev - delta)).astype(jnp.bfloat16)
        ds_ref[prev_span(i, blocks), :] = dscore
        dv = dot(prob.astype(jnp.bfloat16), grad_rows, NN)
        dk = dot(dscore, query_rows, NN)
        if i == 0:
            dv_ref[...] = dv
            dk_ref[...] = dk
        else:
            dv_ref[seen, :] += dv
            dk_ref[seen, :] += dk
        stat_ref[i, 0:1, :] = top
        stat_ref[i, 1:2, :] = inverse
        stat_ref[i, 2:3, :] = delta
    send_ref[:, :HEAD_WIDTH] = (dk_ref[...] * SCALE).astype(jnp.bfloat16)
    send_ref[:, HEAD_WIDTH:] = dv_ref[...].astype(jnp.bfloat16)


def own_kernel(kv_heads, *refs):
    q_ref, g_ref, k_ref, pk_ref, start_ref = refs[:5]
    per_head = [refs[5 + 4 * g : 9 + 4 * g] for g in range(kv_heads)]
    refs = refs[5 + 4 * kv_heads :]
    dq_hbm, keeps, (dq_ref, dk_ref, dv_ref, sems) = refs[0], refs[1 : 1 + kv_heads], refs[1 + kv_heads :]
    rows, width = q_ref.shape
    heads = width // k_ref.shape[1]
    blocks = rows // BLOCK
    copies = []
    for g in range(kv_heads):
        s_ref, d_ref, stat_ref, ds_ref = per_head[g]
        for i in reversed(range(blocks)):
            start = start_ref[:, i * BLOCK : (i + 1) * BLOCK]
            query_rows = stacked(q_ref, i, g, heads)
            grad_rows = stacked(g_ref, i, g, heads)
            seen = slice(0, (i + 1) * BLOCK)
            top, inverse, delta = (stat_ref[i, n : n + 1, :] for n in range(3))
            own = masked(s_ref[own_span(i), :], start, query_row(i), 0, True)
            own = jnp.exp2((own - top) * (SCALE * LOG2E)) * inverse
            down = (own * (d_ref[own_span(i), :] - delta)).astype(jnp.bfloat16)
            dv = dot(own.astype(jnp.bfloat16), grad_rows, NN)
            dk = dot(down, query_rows, NN)
            if i == blocks - 1:
                dv_ref[...] = dv
                dk_ref[...] = dk
            else:
                dv_ref[seen, :] += dv
                dk_ref[seen, :] += dk
            dq = dot(pk_ref[i * BLOCK : rows, column(g)], ds_ref[prev_span(i, blocks), :], TN)
            dq = (dq + dot(k_ref[seen, column(g)], down, TN)) * SCALE
            place = (
                pl.ds(i * BLOCK, BLOCK),
                pl.ds(g * heads * HEAD_WIDTH, heads * HEAD_WIDTH),
            )
            for h in range(heads):
                dq_ref[place[0], pl.ds((g * heads + h) * HEAD_WIDTH, HEAD_WIDTH)] = jnp.transpose(
                    dq[:, h * BLOCK : (h + 1) * BLOCK]
                ).astype(jnp.bfloat16)
            copy = pltpu.make_async_copy(
                dq_ref.at[place], dq_hbm.at[place], sems.at[g * blocks + i]
            )
            copy.start()
            copies.append(copy)
        keeps[g][:, :HEAD_WIDTH] = dk_ref[...] * SCALE
        keeps[g][:, HEAD_WIDTH:] = dv_ref[...]
    for copy in copies:
        copy.wait()


def sum_kernel(kv_heads, *refs):
    keep, back = refs[:kv_heads], refs[kv_heads : 2 * kv_heads]
    dk_ref, dv_ref = refs[2 * kv_heads :]
    for g in range(kv_heads):
        total = keep[g][...] + back[g][...].astype(jnp.float32)
        dk_ref[:, column(g)] = total[:, :HEAD_WIDTH].astype(jnp.bfloat16)
        dv_ref[:, column(g)] = total[:, HEAD_WIDTH:].astype(jnp.bfloat16)


def body(queries, keys, values, output_gradient, doc_lengths):
    rows = queries.shape[0]
    kv_heads = keys.shape[1] // HEAD_WIDTH
    heads = queries.shape[1] // keys.shape[1]
    blocks = rows // BLOCK
    pairs = blocks * (blocks + 1) // 2 * BLOCK
    lanes = heads * BLOCK
    prev_keys = rotated(keys, "seq", 1)
    prev_values = rotated(values, "seq", 1)
    lengths = gathered_lengths(doc_lengths)
    first = (lax.axis_index("seq") * rows).astype(jnp.int32).reshape(1)
    params = pltpu.CompilerParams(vmem_limit_bytes=24 * 1024 * 1024)
    shape = jax.ShapeDtypeStruct
    vmem = pl.BlockSpec(memory_space=pltpu.VMEM)
    pair = shape((rows, 2 * HEAD_WIDTH), jnp.bfloat16)
    scratch = [pltpu.VMEM((rows, HEAD_WIDTH), jnp.float32)] * 2

    raw = pl.pallas_call(
        raw_kernel,
        out_shape=[shape((pairs, lanes), jnp.float32)] * (2 * kv_heads),
        compiler_params=params,
        name="own_products",
    )(queries, output_gradient, keys, values)
    sends, per_head = [], []
    for g in range(kv_heads):
        send, stat, start, ds = pl.pallas_call(
            functools.partial(prev_kernel, g),
            out_shape=(
                pair,
                shape((blocks, 8, lanes), jnp.float32),
                shape((1, rows), jnp.int32),
                shape((pairs, lanes), jnp.bfloat16),
            ),
            in_specs=[pl.BlockSpec(memory_space=pltpu.SMEM)] + [vmem] * 7,
            scratch_shapes=scratch,
            compiler_params=params,
            name="prev_grads",
        )(
            first, lengths, queries, output_gradient, prev_keys, prev_values,
            raw[2 * g], raw[2 * g + 1],
        )
        sends.append(send)
        per_head += [raw[2 * g], raw[2 * g + 1], stat, ds]
    backs = [rotated(send, "seq", -1) for send in sends]
    grad_queries, *keeps = pl.pallas_call(
        functools.partial(own_kernel, kv_heads),
        out_shape=[shape(queries.shape, jnp.bfloat16)]
        + [shape(pair.shape, jnp.float32)] * kv_heads,
        in_specs=[vmem] * (5 + 4 * kv_heads),
        out_specs=[pl.BlockSpec(memory_space=pl.ANY)] + [vmem] * kv_heads,
        scratch_shapes=[pltpu.VMEM(queries.shape, jnp.bfloat16)]
        + scratch
        + [pltpu.SemaphoreType.DMA((kv_heads * blocks,))],
        compiler_params=params,
        name="own_grads",
    )(queries, output_gradient, keys, prev_keys, start, *per_head)
    key_gradient, value_gradient = pl.pallas_call(
        functools.partial(sum_kernel, kv_heads),
        out_shape=[shape(keys.shape, jnp.bfloat16)] * 2,
        compiler_params=params,
        name="sums",
    )(*keeps, *backs)
    return (grad_queries, key_gradient, value_gradient)


def solution(mesh):
    in_specs = (
        P("seq", "head"),
        P("seq", "head"),
        P("seq", "head"),
        P("seq", "head"),
        P(("seq", "head")),
    )
    out_specs = (P("seq", "head"), P("seq", "head"), P("seq", "head"))
    return jax.shard_map(body, mesh=mesh, in_specs=in_specs, out_specs=out_specs, check_vma=False)
```

```python
import functools

import jax
import jax.numpy as jnp
from jax import lax
from jax.experimental import pallas as pl
from jax.experimental.pallas import tpu as pltpu
from jax.sharding import PartitionSpec as P

HEAD_WIDTH = 128
BLOCK = 128
SCALE = HEAD_WIDTH ** (-0.5)
LOG2E = 1.4426950408889634
NT = (((1,), (1,)), ((), ()))
NN = (((1,), (0,)), ((), ()))
TN = (((0,), (0,)), ((), ()))


def dot(a, b, dims):
    return lax.dot_general(a, b, dims, preferred_element_type=jnp.float32)


def rotated(value, axis, steps):
    count = lax.axis_size(axis)
    return lax.ppermute(value, axis, [(s, (s + steps) % count) for s in range(count)])


def round_groups(axes):
    count = lax.axis_size(axes)
    bits = [1 << b for b in range(1, count.bit_length() - 1)]
    return [bits[n : n + 2] for n in range(0, len(bits), 2)] + [[1]]


def summed_round(value, axes, group):
    count = lax.axis_size(axes)
    masks = group + [sum(group)] * (len(group) - 1)
    others = [lax.ppermute(value, axes, [(s, s ^ m) for s in range(count)]) for m in masks]
    return functools.reduce(jnp.add, others, value)


def lengths_row(doc_lengths, axes):
    own = doc_lengths.shape[0]
    shards = lax.axis_size(axes)
    spot = lax.broadcasted_iota(jnp.int32, (1, shards, own), 1) == lax.axis_index(axes)
    return jnp.where(spot, doc_lengths[None, None, :], 0).reshape(1, shards * own)


def start_row(lengths, first, rows):
    docs = lengths.shape[1]
    before = lax.broadcasted_iota(jnp.int32, (docs, docs), 1) < lax.broadcasted_iota(
        jnp.int32, (docs, docs), 0
    )
    starts = jnp.sum(
        jnp.where(before, jnp.broadcast_to(lengths, (docs, docs)), 0), axis=1, keepdims=True
    )
    starts = jnp.broadcast_to(starts - first, (docs, rows))
    own = lax.broadcasted_iota(jnp.int32, (docs, rows), 1)
    return jnp.max(jnp.where(starts <= own, starts, -first), axis=0, keepdims=True)


def stacked(ref, i, g, heads):
    return jnp.concatenate(
        [
            ref[pl.ds(i * BLOCK, BLOCK), pl.ds((g * heads + h) * HEAD_WIDTH, HEAD_WIDTH)]
            for h in range(heads)
        ],
        axis=0,
    )


def masked(scores, start, first_key, query=None):
    key = first_key + lax.broadcasted_iota(jnp.int32, (scores.shape[0], BLOCK), 0)
    allowed = key >= start
    if query is not None:
        allowed = allowed & (key <= query)
    return jnp.concatenate(
        [
            jnp.where(allowed, scores[:, c : c + BLOCK], -jnp.inf)
            for c in range(0, scores.shape[1], BLOCK)
        ],
        axis=1,
    )


def own_span(i):
    return slice(i * (i + 1) // 2 * BLOCK, (i + 1) * (i + 2) // 2 * BLOCK)


def own_scores(s_ref, start_ref, i):
    at = slice(i * BLOCK, (i + 1) * BLOCK)
    query = i * BLOCK + lax.broadcasted_iota(jnp.int32, (1, BLOCK), 1)
    return masked(s_ref[own_span(i), :], start_ref[:, at], 0, query)


def column(g):
    return slice(g * HEAD_WIDTH, (g + 1) * HEAD_WIDTH)


def raw_kernel(after_ref, q_hbm, g_hbm, k_hbm, v_hbm, zero_ref, q_ref, g_ref, k_ref, v_ref, *outs):
    outs, sems = outs[:-1], outs[-1]
    rows, width = q_ref.shape
    kv_heads = k_ref.shape[1] // HEAD_WIDTH
    heads = width // k_ref.shape[1]
    blocks = rows // BLOCK

    def fetch(n, source, target, at):
        copy = pltpu.make_async_copy(source.at[at], target.at[at], sems.at[n])
        copy.start()
        return copy

    zero_ref[...] = jnp.zeros(zero_ref.shape, jnp.int32)
    whole = pl.ds(0, rows)
    first = [fetch(0, k_hbm, k_ref, whole), fetch(1, v_hbm, v_ref, whole)]
    parts = [
        [
            fetch(2 + 2 * i, q_hbm, q_ref, pl.ds(i * BLOCK, BLOCK)),
            fetch(3 + 2 * i, g_hbm, g_ref, pl.ds(i * BLOCK, BLOCK)),
        ]
        for i in range(blocks)
    ]
    for copy in first:
        copy.wait()
    for i in range(blocks):
        for copy in parts[i]:
            copy.wait()
        seen = slice(0, (i + 1) * BLOCK)
        for g in range(kv_heads):
            s_ref, d_ref = outs[2 * g : 2 * g + 2]
            scores = dot(k_ref[seen, column(g)], stacked(q_ref, i, g, heads), NT)
            s_ref[own_span(i), :] = scores * (SCALE * LOG2E)
            d_ref[own_span(i), :] = dot(v_ref[seen, column(g)], stacked(g_ref, i, g, heads), NT)


def prev_kernel(
    g, first_ref, len_ref, q_ref, g_ref, pk_ref, pv_ref, s_ref, d_ref,
    send_ref, stat_ref, start_ref, dq_ref, reach_ref,
):
    rows, width = q_ref.shape
    heads = width // pk_ref.shape[1]
    blocks = rows // BLOCK
    start = start_row(len_ref[...], first_ref[0], rows)
    start_ref[...] = start
    before = pl.cdiv(jnp.maximum(-jnp.min(start), 0), BLOCK)
    after = pl.cdiv(jnp.sum((start < 0).astype(jnp.int32)), BLOCK)
    reach_ref[0] = after
    for i in range(blocks):
        own = own_scores(s_ref, start_ref, i)
        top = jnp.max(own, axis=0, keepdims=True)
        own = jnp.exp2(own - top)
        stat_ref[i, 0:1, :] = top
        stat_ref[i, 1:2, :] = jnp.sum(own, axis=0, keepdims=True)
        stat_ref[i, 2:3, :] = jnp.sum(own * d_ref[own_span(i), :], axis=0, keepdims=True)

    def crossing(keys, queries):
        seen = slice((blocks - keys) * BLOCK, rows)
        key_rows, value_rows = pk_ref[seen, column(g)], pv_ref[seen, column(g)]
        probs, dscores, query_rows, grad_rows = [], [], [], []
        for i in range(queries):
            query_rows.append(stacked(q_ref, i, g, heads))
            grad_rows.append(stacked(g_ref, i, g, heads))
            prev = dot(key_rows, query_rows[i], NT) * (SCALE * LOG2E)
            prev = masked(prev, start_ref[:, i * BLOCK : (i + 1) * BLOCK], -keys * BLOCK)
            own_top, own_total, own_sum = (stat_ref[i, n : n + 1, :] for n in range(3))
            top = jnp.maximum(own_top, jnp.max(prev, axis=0, keepdims=True))
            prev = jnp.exp2(prev - top)
            kept = jnp.exp2(own_top - top)
            dprev = dot(value_rows, grad_rows[i], NT)
            total = own_total * kept + jnp.sum(prev, axis=0, keepdims=True)
            dsum = own_sum * kept + jnp.sum(prev * dprev, axis=0, keepdims=True)
            stat_ref[i, 0:1, :] = top
            stat_ref[i, 1:2, :] = total
            stat_ref[i, 2:3, :] = dsum
            inverse = 1.0 / total
            prob = prev * inverse
            dscore = (prob * (dprev - dsum * inverse)).astype(jnp.bfloat16)
            probs.append(prob.astype(jnp.bfloat16))
            dscores.append(dscore)
        probs, dscores = (jnp.concatenate(x, axis=1) for x in (probs, dscores))
        query_rows, grad_rows = (jnp.concatenate(x, axis=0) for x in (query_rows, grad_rows))
        send_ref[seen, HEAD_WIDTH:] = dot(probs, grad_rows, NN).astype(jnp.bfloat16)
        send_ref[seen, :HEAD_WIDTH] = (dot(dscores, query_rows, NN) * SCALE).astype(jnp.bfloat16)
        dq = dot(key_rows, dscores, TN)
        for i in range(queries):
            dq_ref[i] = dq[:, i * heads * BLOCK : (i + 1) * heads * BLOCK]
        if keys < blocks:
            rest = slice(0, (blocks - keys) * BLOCK)
            send_ref[rest, :] = jnp.zeros(send_ref[rest, :].shape, jnp.bfloat16)

    for keys in range(1, blocks + 1):
        for queries in range(1, blocks + 2 - keys):
            pl.when((before == keys) & (after == queries))(
                functools.partial(crossing, keys, queries)
            )

    @pl.when(after == 0)
    def _():
        send_ref[...] = jnp.zeros(send_ref.shape, jnp.bfloat16)


def own_kernel(kv_heads, *refs):
    reach_ref, q_ref, g_ref, k_ref, start_ref = refs[:5]
    per_head = [refs[5 + 4 * g : 9 + 4 * g] for g in range(kv_heads)]
    refs = refs[5 + 4 * kv_heads :]
    dq_hbm, keeps, (dq_ref, dk_ref, dv_ref, sems) = refs[0], refs[1 : 1 + kv_heads], refs[1 + kv_heads :]
    rows, width = q_ref.shape
    heads = width // k_ref.shape[1]
    blocks = rows // BLOCK
    reach = reach_ref[0]
    copies = []
    for g in range(kv_heads):
        s_ref, d_ref, stat_ref, dqp_ref = per_head[g]
        for i in reversed(range(blocks)):
            query_rows = stacked(q_ref, i, g, heads)
            grad_rows = stacked(g_ref, i, g, heads)
            seen = slice(0, (i + 1) * BLOCK)
            top, total, dsum = (stat_ref[i, n : n + 1, :] for n in range(3))
            inverse = 1.0 / total
            own = jnp.exp2(own_scores(s_ref, start_ref, i) - top) * inverse
            down = (own * (d_ref[own_span(i), :] - dsum * inverse)).astype(jnp.bfloat16)
            dv = dot(own.astype(jnp.bfloat16), grad_rows, NN)
            dk = dot(down, query_rows, NN)
            if i == blocks - 1:
                dv_ref[...] = dv
                dk_ref[...] = dk
            else:
                dv_ref[seen, :] += dv
                dk_ref[seen, :] += dk
            dq = dot(k_ref[seen, column(g)], down, TN)
            dq = (dq + jnp.where(i < reach, dqp_ref[i], 0.0)) * SCALE
            place = (
                pl.ds(i * BLOCK, BLOCK),
                pl.ds(g * heads * HEAD_WIDTH, heads * HEAD_WIDTH),
            )
            for h in range(heads):
                dq_ref[place[0], pl.ds((g * heads + h) * HEAD_WIDTH, HEAD_WIDTH)] = jnp.transpose(
                    dq[:, h * BLOCK : (h + 1) * BLOCK]
                ).astype(jnp.bfloat16)
            copy = pltpu.make_async_copy(
                dq_ref.at[place], dq_hbm.at[place], sems.at[g * blocks + i]
            )
            copy.start()
            copies.append(copy)
        keeps[g][:, :HEAD_WIDTH] = dk_ref[...] * SCALE
        keeps[g][:, HEAD_WIDTH:] = dv_ref[...]
    for copy in copies:
        copy.wait()


def sum_kernel(kv_heads, *refs):
    keep, back = refs[:kv_heads], refs[kv_heads : 2 * kv_heads]
    dk_ref, dv_ref = refs[2 * kv_heads :]
    for g in range(kv_heads):
        total = keep[g][...] + back[g][...].astype(jnp.float32)
        dk_ref[:, column(g)] = total[:, :HEAD_WIDTH].astype(jnp.bfloat16)
        dv_ref[:, column(g)] = total[:, HEAD_WIDTH:].astype(jnp.bfloat16)


def body(queries, keys, values, output_gradient, doc_lengths):
    rows = queries.shape[0]
    kv_heads = keys.shape[1] // HEAD_WIDTH
    heads = queries.shape[1] // keys.shape[1]
    blocks = rows // BLOCK
    pairs = blocks * (blocks + 1) // 2 * BLOCK
    lanes = heads * BLOCK
    prev_keys = rotated(keys, "seq", 1)
    prev_values = rotated(values, "seq", 1)
    axes = ("seq", "head")
    groups = round_groups(axes)
    row = summed_round(lengths_row(doc_lengths, axes), axes, groups[0])
    first = (lax.axis_index("seq") * rows).astype(jnp.int32).reshape(1)
    params = pltpu.CompilerParams(vmem_limit_bytes=24 * 1024 * 1024)
    shape = jax.ShapeDtypeStruct
    vmem = pl.BlockSpec(memory_space=pltpu.VMEM)
    smem = pl.BlockSpec(memory_space=pltpu.SMEM)
    hbm = pl.BlockSpec(memory_space=pltpu.HBM)
    pair = shape((rows, 2 * HEAD_WIDTH), jnp.bfloat16)
    scratch = [pltpu.VMEM((rows, HEAD_WIDTH), jnp.float32)] * 2

    arrays = (queries, output_gradient, keys, values)
    zero, q, g_out, k, v, *raw = pl.pallas_call(
        raw_kernel,
        out_shape=[shape(row.shape, jnp.int32)]
        + [pltpu.VMEM(a.shape, a.dtype) for a in arrays]
        + [pltpu.VMEM((pairs, lanes), jnp.float32)] * (2 * kv_heads),
        in_specs=[hbm] * 5,
        out_specs=[vmem] * (5 + 2 * kv_heads),
        scratch_shapes=[pltpu.SemaphoreType.DMA((2 + 2 * blocks,))],
        compiler_params=params,
        name="own_products",
    )(row, *(pltpu.with_memory_space_constraint(a, pltpu.HBM) for a in arrays))
    for n, group in enumerate(groups[1:]):
        if n == len(groups) - 2:
            row = row + zero
        row = summed_round(row, axes, group)
    sends, per_head = [], []
    for g in range(kv_heads):
        send, stat, start, dq, reach = pl.pallas_call(
            functools.partial(prev_kernel, g),
            out_shape=(
                pair,
                shape((blocks, 8, lanes), jnp.float32),
                shape((1, rows), jnp.int32),
                shape((blocks, HEAD_WIDTH, lanes), jnp.float32),
                shape((1,), jnp.int32),
            ),
            in_specs=[smem] + [vmem] * 7,
            out_specs=[vmem] * 4 + [smem],
            compiler_params=params,
            name="prev_grads",
        )(first, row, q, g_out, prev_keys, prev_values, raw[2 * g], raw[2 * g + 1])
        sends.append(send)
        per_head += [raw[2 * g], raw[2 * g + 1], stat, dq]
    backs = [rotated(send, "seq", -1) for send in sends]
    grad_queries, *keeps = pl.pallas_call(
        functools.partial(own_kernel, kv_heads),
        out_shape=[shape(queries.shape, jnp.bfloat16)]
        + [shape(pair.shape, jnp.float32)] * kv_heads,
        in_specs=[smem] + [vmem] * (4 + 4 * kv_heads),
        out_specs=[hbm] + [vmem] * kv_heads,
        scratch_shapes=[pltpu.VMEM(queries.shape, jnp.bfloat16)]
        + scratch
        + [pltpu.SemaphoreType.DMA((kv_heads * blocks,))],
        compiler_params=params,
        name="own_grads",
    )(reach, q, g_out, k, start, *per_head)
    key_gradient, value_gradient = pl.pallas_call(
        functools.partial(sum_kernel, kv_heads),
        out_shape=[shape(keys.shape, jnp.bfloat16)] * 2,
        compiler_params=params,
        name="sums",
    )(*keeps, *backs)
    return (grad_queries, key_gradient, value_gradient)


def solution(mesh):
    in_specs = (
        P("seq", "head"),
        P("seq", "head"),
        P("seq", "head"),
        P("seq", "head"),
        P(("seq", "head")),
    )
    out_specs = (P("seq", "head"), P("seq", "head"), P("seq", "head"))
    return jax.shard_map(body, mesh=mesh, in_specs=in_specs, out_specs=out_specs, check_vma=False)
```

```python
import functools

import jax
import jax.numpy as jnp
from jax import lax
from jax.experimental import pallas as pl
from jax.experimental.pallas import tpu as pltpu
from jax.sharding import PartitionSpec as P

HEAD_WIDTH = 128
BLOCK = 128
SCALE = HEAD_WIDTH ** (-0.5)
LOG2E = 1.4426950408889634
NT = (((1,), (1,)), ((), ()))
NN = (((1,), (0,)), ((), ()))
TN = (((0,), (0,)), ((), ()))


def dot(a, b, dims):
    return lax.dot_general(a, b, dims, preferred_element_type=jnp.float32)


def rotated(value, axis, steps):
    count = lax.axis_size(axis)
    return lax.ppermute(value, axis, [(s, (s + steps) % count) for s in range(count)])


def round_groups(axes):
    count = lax.axis_size(axes)
    bits = [1 << b for b in range(1, count.bit_length() - 1)]
    return [bits[n : n + 2] for n in range(0, len(bits), 2)] + [[1]]


def summed_round(value, axes, group):
    count = lax.axis_size(axes)
    masks = group + [sum(group)] * (len(group) - 1)
    others = [lax.ppermute(value, axes, [(s, s ^ m) for s in range(count)]) for m in masks]
    return functools.reduce(jnp.add, others, value)


def lengths_row(doc_lengths, axes):
    own = doc_lengths.shape[0]
    shards = lax.axis_size(axes)
    spot = lax.broadcasted_iota(jnp.int32, (1, shards, own), 1) == lax.axis_index(axes)
    return jnp.where(spot, doc_lengths[None, None, :], 0).reshape(1, shards * own)


def start_row(lengths, first, rows):
    docs = lengths.shape[1]
    before = lax.broadcasted_iota(jnp.int32, (docs, docs), 1) < lax.broadcasted_iota(
        jnp.int32, (docs, docs), 0
    )
    starts = jnp.sum(
        jnp.where(before, jnp.broadcast_to(lengths, (docs, docs)), 0), axis=1, keepdims=True
    )
    starts = jnp.broadcast_to(starts - first, (docs, rows))
    own = lax.broadcasted_iota(jnp.int32, (docs, rows), 1)
    return jnp.max(jnp.where(starts <= own, starts, -first), axis=0, keepdims=True)


def stacked(ref, i, g, heads):
    return jnp.concatenate(
        [
            ref[pl.ds(i * BLOCK, BLOCK), pl.ds((g * heads + h) * HEAD_WIDTH, HEAD_WIDTH)]
            for h in range(heads)
        ],
        axis=0,
    )


def masked(scores, start, first_key, query=None):
    key = first_key + lax.broadcasted_iota(jnp.int32, (scores.shape[0], BLOCK), 0)
    allowed = key >= start
    if query is not None:
        allowed = allowed & (key <= query)
    return jnp.concatenate(
        [
            jnp.where(allowed, scores[:, c : c + BLOCK], -jnp.inf)
            for c in range(0, scores.shape[1], BLOCK)
        ],
        axis=1,
    )


def own_span(i):
    return slice(i * (i + 1) // 2 * BLOCK, (i + 1) * (i + 2) // 2 * BLOCK)


def own_scores(s_ref, start_ref, i):
    at = slice(i * BLOCK, (i + 1) * BLOCK)
    query = i * BLOCK + lax.broadcasted_iota(jnp.int32, (1, BLOCK), 1)
    return masked(s_ref[own_span(i), :], start_ref[:, at], 0, query)


def column(g):
    return slice(g * HEAD_WIDTH, (g + 1) * HEAD_WIDTH)


def raw_kernel(after_ref, q_hbm, g_hbm, k_hbm, v_hbm, zero_ref, q_ref, g_ref, k_ref, *outs):
    outs, v_ref, sems = outs[:-2], outs[-2], outs[-1]
    rows, width = q_ref.shape
    kv_heads = k_ref.shape[1] // HEAD_WIDTH
    heads = width // k_ref.shape[1]
    blocks = rows // BLOCK

    def fetch(n, source, target, at):
        copy = pltpu.make_async_copy(source.at[at], target.at[at], sems.at[n])
        copy.start()
        return copy

    zero_ref[...] = jnp.zeros(zero_ref.shape, jnp.int32)
    whole = pl.ds(0, rows)
    first = [fetch(0, k_hbm, k_ref, whole), fetch(1, v_hbm, v_ref, whole)]
    parts = [
        [
            fetch(2 + 2 * i, q_hbm, q_ref, pl.ds(i * BLOCK, BLOCK)),
            fetch(3 + 2 * i, g_hbm, g_ref, pl.ds(i * BLOCK, BLOCK)),
        ]
        for i in range(blocks)
    ]
    for copy in first:
        copy.wait()
    for i in range(blocks):
        for copy in parts[i]:
            copy.wait()
        seen = slice(0, (i + 1) * BLOCK)
        for g in range(kv_heads):
            s_ref, d_ref = outs[2 * g : 2 * g + 2]
            scores = dot(k_ref[seen, column(g)], stacked(q_ref, i, g, heads), NT)
            s_ref[own_span(i), :] = scores * (SCALE * LOG2E)
            d_ref[own_span(i), :] = dot(v_ref[seen, column(g)], stacked(g_ref, i, g, heads), NT)


def prev_kernel(
    g, first_ref, len_ref, q_ref, g_ref, pk_ref, pv_ref, s_ref, d_ref,
    send_ref, stat_ref, start_ref, dq_ref, reach_ref,
):
    rows, width = q_ref.shape
    heads = width // pk_ref.shape[1]
    blocks = rows // BLOCK
    start = start_row(len_ref[...], first_ref[0], rows)
    start_ref[...] = start
    before = pl.cdiv(jnp.maximum(-jnp.min(start), 0), BLOCK)
    after = pl.cdiv(jnp.sum((start < 0).astype(jnp.int32)), BLOCK)
    reach_ref[0] = after
    for i in range(blocks):
        own = own_scores(s_ref, start_ref, i)
        top = jnp.max(own, axis=0, keepdims=True)
        own = jnp.exp2(own - top)
        stat_ref[i, 0:1, :] = top
        stat_ref[i, 1:2, :] = jnp.sum(own, axis=0, keepdims=True)
        stat_ref[i, 2:3, :] = jnp.sum(own * d_ref[own_span(i), :], axis=0, keepdims=True)

    def crossing(keys, queries):
        seen = slice((blocks - keys) * BLOCK, rows)
        key_rows, value_rows = pk_ref[seen, column(g)], pv_ref[seen, column(g)]
        probs, dscores, query_rows, grad_rows = [], [], [], []
        for i in range(queries):
            query_rows.append(stacked(q_ref, i, g, heads))
            grad_rows.append(stacked(g_ref, i, g, heads))
            prev = dot(key_rows, query_rows[i], NT) * (SCALE * LOG2E)
            prev = masked(prev, start_ref[:, i * BLOCK : (i + 1) * BLOCK], -keys * BLOCK)
            own_top, own_total, own_sum = (stat_ref[i, n : n + 1, :] for n in range(3))
            top = jnp.maximum(own_top, jnp.max(prev, axis=0, keepdims=True))
            prev = jnp.exp2(prev - top)
            kept = jnp.exp2(own_top - top)
            dprev = dot(value_rows, grad_rows[i], NT)
            total = own_total * kept + jnp.sum(prev, axis=0, keepdims=True)
            dsum = own_sum * kept + jnp.sum(prev * dprev, axis=0, keepdims=True)
            stat_ref[i, 0:1, :] = top
            stat_ref[i, 1:2, :] = total
            stat_ref[i, 2:3, :] = dsum
            inverse = 1.0 / total
            prob = prev * inverse
            dscore = (prob * (dprev - dsum * inverse)).astype(jnp.bfloat16)
            probs.append(prob.astype(jnp.bfloat16))
            dscores.append(dscore)
        probs, dscores = (jnp.concatenate(x, axis=1) for x in (probs, dscores))
        query_rows, grad_rows = (jnp.concatenate(x, axis=0) for x in (query_rows, grad_rows))
        send_ref[seen, HEAD_WIDTH:] = dot(probs, grad_rows, NN).astype(jnp.bfloat16)
        send_ref[seen, :HEAD_WIDTH] = (dot(dscores, query_rows, NN) * SCALE).astype(jnp.bfloat16)
        dq = dot(key_rows, dscores, TN)
        for i in range(queries):
            dq_ref[i] = dq[:, i * heads * BLOCK : (i + 1) * heads * BLOCK]
        if keys < blocks:
            rest = slice(0, (blocks - keys) * BLOCK)
            send_ref[rest, :] = jnp.zeros(send_ref[rest, :].shape, jnp.bfloat16)

    for keys in range(1, blocks + 1):
        for queries in range(1, blocks + 2 - keys):
            pl.when((before == keys) & (after == queries))(
                functools.partial(crossing, keys, queries)
            )

    @pl.when(after == 0)
    def _():
        send_ref[...] = jnp.zeros(send_ref.shape, jnp.bfloat16)


def own_kernel(kv_heads, *refs):
    reach_ref, q_ref, g_ref, k_ref, start_ref = refs[:5]
    per_head = [refs[5 + 4 * g : 9 + 4 * g] for g in range(kv_heads)]
    refs = refs[5 + 4 * kv_heads :]
    dq_hbm, keeps, (dq_ref, dk_ref, dv_ref, sems) = refs[0], refs[1 : 1 + kv_heads], refs[1 + kv_heads :]
    rows, width = q_ref.shape
    heads = width // k_ref.shape[1]
    blocks = rows // BLOCK
    reach = reach_ref[0]
    copies = []
    for g in range(kv_heads):
        s_ref, d_ref, stat_ref, dqp_ref = per_head[g]
        for i in reversed(range(blocks)):
            query_rows = stacked(q_ref, i, g, heads)
            grad_rows = stacked(g_ref, i, g, heads)
            seen = slice(0, (i + 1) * BLOCK)
            top, total, dsum = (stat_ref[i, n : n + 1, :] for n in range(3))
            inverse = 1.0 / total
            own = jnp.exp2(own_scores(s_ref, start_ref, i) - top) * inverse
            down = (own * (d_ref[own_span(i), :] - dsum * inverse)).astype(jnp.bfloat16)
            dv = dot(own.astype(jnp.bfloat16), grad_rows, NN)
            dk = dot(down, query_rows, NN)
            if i == blocks - 1:
                dv_ref[...] = dv
                dk_ref[...] = dk
            else:
                dv_ref[seen, :] += dv
                dk_ref[seen, :] += dk
            dq = dot(k_ref[seen, column(g)], down, TN)
            dq = (dq + jnp.where(i < reach, dqp_ref[i], 0.0)) * SCALE
            place = (
                pl.ds(i * BLOCK, BLOCK),
                pl.ds(g * heads * HEAD_WIDTH, heads * HEAD_WIDTH),
            )
            for h in range(heads):
                dq_ref[place[0], pl.ds((g * heads + h) * HEAD_WIDTH, HEAD_WIDTH)] = jnp.transpose(
                    dq[:, h * BLOCK : (h + 1) * BLOCK]
                ).astype(jnp.bfloat16)
            copy = pltpu.make_async_copy(
                dq_ref.at[place], dq_hbm.at[place], sems.at[g * blocks + i]
            )
            copy.start()
            copies.append(copy)
        keeps[g][:, :HEAD_WIDTH] = dk_ref[...] * SCALE
        keeps[g][:, HEAD_WIDTH:] = dv_ref[...]
    for copy in copies:
        copy.wait()


def sum_kernel(kv_heads, *refs):
    keep, back = refs[:kv_heads], refs[kv_heads : 2 * kv_heads]
    dk_ref, dv_ref = refs[2 * kv_heads :]
    for g in range(kv_heads):
        total = keep[g][...] + back[g][...].astype(jnp.float32)
        dk_ref[:, column(g)] = total[:, :HEAD_WIDTH].astype(jnp.bfloat16)
        dv_ref[:, column(g)] = total[:, HEAD_WIDTH:].astype(jnp.bfloat16)


def body(queries, keys, values, output_gradient, doc_lengths):
    rows = queries.shape[0]
    kv_heads = keys.shape[1] // HEAD_WIDTH
    heads = queries.shape[1] // keys.shape[1]
    blocks = rows // BLOCK
    pairs = blocks * (blocks + 1) // 2 * BLOCK
    lanes = heads * BLOCK
    prev_keys = rotated(keys, "seq", 1)
    prev_values = rotated(values, "seq", 1)
    axes = ("seq", "head")
    groups = round_groups(axes)
    row = summed_round(lengths_row(doc_lengths, axes), axes, groups[0])
    first = (lax.axis_index("seq") * rows).astype(jnp.int32).reshape(1)
    params = pltpu.CompilerParams(vmem_limit_bytes=24 * 1024 * 1024)
    shape = jax.ShapeDtypeStruct
    vmem = pl.BlockSpec(memory_space=pltpu.VMEM)
    smem = pl.BlockSpec(memory_space=pltpu.SMEM)
    hbm = pl.BlockSpec(memory_space=pltpu.HBM)
    pair = shape((rows, 2 * HEAD_WIDTH), jnp.bfloat16)
    scratch = [pltpu.VMEM((rows, HEAD_WIDTH), jnp.float32)] * 2

    arrays = (queries, output_gradient, keys, values)
    zero, q, g_out, k, *raw = pl.pallas_call(
        raw_kernel,
        out_shape=[shape(row.shape, jnp.int32)]
        + [shape(a.shape, a.dtype) for a in arrays[:3]]
        + [shape((pairs, lanes), jnp.float32)] * (2 * kv_heads),
        in_specs=[hbm] * 5,
        out_specs=[vmem] * (4 + 2 * kv_heads),
        scratch_shapes=[
            pltpu.VMEM(values.shape, values.dtype),
            pltpu.SemaphoreType.DMA((2 + 2 * blocks,)),
        ],
        compiler_params=params,
        name="own_products",
    )(row, *(pltpu.with_memory_space_constraint(a, pltpu.HBM) for a in arrays))
    for n, group in enumerate(groups[1:]):
        if n == len(groups) - 2:
            row = row + zero
        row = summed_round(row, axes, group)
    sends, per_head = [], []
    for g in range(kv_heads):
        send, stat, start, dq, reach = pl.pallas_call(
            functools.partial(prev_kernel, g),
            out_shape=(
                pair,
                shape((blocks, 8, lanes), jnp.float32),
                shape((1, rows), jnp.int32),
                shape((blocks, HEAD_WIDTH, lanes), jnp.float32),
                shape((1,), jnp.int32),
            ),
            in_specs=[smem] + [vmem] * 7,
            out_specs=[vmem] * 4 + [smem],
            compiler_params=params,
            name="prev_grads",
        )(first, row, q, g_out, prev_keys, prev_values, raw[2 * g], raw[2 * g + 1])
        sends.append(send)
        per_head += [raw[2 * g], raw[2 * g + 1], stat, dq]
    backs = [rotated(send, "seq", -1) for send in sends]
    grad_queries, *keeps = pl.pallas_call(
        functools.partial(own_kernel, kv_heads),
        out_shape=[shape(queries.shape, jnp.bfloat16)]
        + [shape(pair.shape, jnp.float32)] * kv_heads,
        in_specs=[smem] + [vmem] * (4 + 4 * kv_heads),
        out_specs=[hbm] + [vmem] * kv_heads,
        scratch_shapes=[pltpu.VMEM(queries.shape, jnp.bfloat16)]
        + scratch
        + [pltpu.SemaphoreType.DMA((kv_heads * blocks,))],
        compiler_params=params,
        name="own_grads",
    )(reach, q, g_out, k, start, *per_head)
    key_gradient, value_gradient = pl.pallas_call(
        functools.partial(sum_kernel, kv_heads),
        out_shape=[shape(keys.shape, jnp.bfloat16)] * 2,
        compiler_params=params,
        name="sums",
    )(*keeps, *backs)
    return (grad_queries, key_gradient, value_gradient)


def solution(mesh):
    in_specs = (
        P("seq", "head"),
        P("seq", "head"),
        P("seq", "head"),
        P("seq", "head"),
        P(("seq", "head")),
    )
    out_specs = (P("seq", "head"), P("seq", "head"), P("seq", "head"))
    return jax.shard_map(body, mesh=mesh, in_specs=in_specs, out_specs=out_specs, check_vma=False)
```

```python
import functools

import jax
import jax.numpy as jnp
from jax import lax
from jax.experimental import pallas as pl
from jax.experimental.pallas import tpu as pltpu
from jax.sharding import PartitionSpec as P

HEAD_WIDTH = 128
BLOCK = 128
SCALE = HEAD_WIDTH ** (-0.5)
LOG2E = 1.4426950408889634
NT = (((1,), (1,)), ((), ()))
NN = (((1,), (0,)), ((), ()))
TN = (((0,), (0,)), ((), ()))


def dot(a, b, dims):
    return lax.dot_general(a, b, dims, preferred_element_type=jnp.float32)


def rotated(value, axis, steps):
    count = lax.axis_size(axis)
    return lax.ppermute(value, axis, [(s, (s + steps) % count) for s in range(count)])


def round_groups():
    low = lax.axis_size("head")
    count = low * lax.axis_size("seq")
    bits = [1 << b for b in range(count.bit_length() - 1)]
    head, seq = [b for b in bits if b < low], [b for b in bits if b > low]
    return [[low]] + [part[n : n + 2] for part in (head, seq) for n in range(0, len(part), 2)]


def summed_round(value, axes, group):
    count = lax.axis_size(axes)
    masks = group + [sum(group)] * (len(group) - 1)
    others = [lax.ppermute(value, axes, [(s, s ^ m) for s in range(count)]) for m in masks]
    return functools.reduce(jnp.add, others, value)


def lengths_row(doc_lengths, axes):
    own = doc_lengths.shape[0]
    shards = lax.axis_size(axes)
    spot = lax.broadcasted_iota(jnp.int32, (1, shards, own), 1) == lax.axis_index(axes)
    return jnp.where(spot, doc_lengths[None, None, :], 0).reshape(1, shards * own)


def start_row(lengths, first, rows):
    docs = lengths.shape[1]
    before = lax.broadcasted_iota(jnp.int32, (docs, docs), 1) < lax.broadcasted_iota(
        jnp.int32, (docs, docs), 0
    )
    starts = jnp.sum(
        jnp.where(before, jnp.broadcast_to(lengths, (docs, docs)), 0), axis=1, keepdims=True
    )
    starts = jnp.broadcast_to(starts - first, (docs, rows))
    own = lax.broadcasted_iota(jnp.int32, (docs, rows), 1)
    return jnp.max(jnp.where(starts <= own, starts, -first), axis=0, keepdims=True)


def stacked(ref, i, g, heads):
    return jnp.concatenate(
        [
            ref[pl.ds(i * BLOCK, BLOCK), pl.ds((g * heads + h) * HEAD_WIDTH, HEAD_WIDTH)]
            for h in range(heads)
        ],
        axis=0,
    )


def masked(scores, start, first_key, query=None):
    key = first_key + lax.broadcasted_iota(jnp.int32, (scores.shape[0], BLOCK), 0)
    allowed = key >= start
    if query is not None:
        allowed = allowed & (key <= query)
    return jnp.concatenate(
        [
            jnp.where(allowed, scores[:, c : c + BLOCK], -jnp.inf)
            for c in range(0, scores.shape[1], BLOCK)
        ],
        axis=1,
    )


def column(g):
    return slice(g * HEAD_WIDTH, (g + 1) * HEAD_WIDTH)


def own_block(i, g, heads, q_ref, g_ref, k_ref, v_ref, start_ref):
    at, seen = slice(i * BLOCK, (i + 1) * BLOCK), slice(0, (i + 1) * BLOCK)
    query_rows, grad_rows = stacked(q_ref, i, g, heads), stacked(g_ref, i, g, heads)
    query = i * BLOCK + lax.broadcasted_iota(jnp.int32, (1, BLOCK), 1)
    scores = dot(k_ref[seen, column(g)], query_rows, NT) * (SCALE * LOG2E)
    scores = masked(scores, start_ref[:, at], 0, query)
    return query_rows, grad_rows, scores, dot(v_ref[seen, column(g)], grad_rows, NT)


def fetch_kernel(count, *refs):
    sources, targets, sems = refs[:count], refs[count : 2 * count], refs[2 * count]
    half = sources[0].shape[0] // 2
    copies = []
    for source, target in zip(sources, targets):
        for at in (pl.ds(0, half), pl.ds(half, half)):
            copies.append(
                pltpu.make_async_copy(source.at[at], target.at[at], sems.at[len(copies)])
            )
            copies[-1].start()
    for copy in copies:
        copy.wait()


def prev_kernel(g, first_ref, len_ref, pk_ref, pv_ref, *refs):
    q_ref, g_ref, k_ref, v_ref = refs[:4]
    if g == 0:
        send_ref, stat_ref, dq_ref, reach_ref, start_ref = refs[4:]
    else:
        start_ref, send_ref, stat_ref, dq_ref = refs[4:]
    rows, width = q_ref.shape
    heads = width // k_ref.shape[1]
    blocks = rows // BLOCK
    if g == 0:
        start_ref[...] = start_row(len_ref[...], first_ref[0], rows)
    start = start_ref[...]
    before = pl.cdiv(jnp.maximum(-jnp.min(start), 0), BLOCK)
    after = pl.cdiv(jnp.sum((start < 0).astype(jnp.int32)), BLOCK)
    if g == 0:
        reach_ref[0] = after
    for i in range(blocks):
        _, _, own, down = own_block(i, g, heads, q_ref, g_ref, k_ref, v_ref, start_ref)
        top = jnp.max(own, axis=0, keepdims=True)
        own = jnp.exp2(own - top)
        stat_ref[i, 0:1, :] = top
        stat_ref[i, 1:2, :] = jnp.sum(own, axis=0, keepdims=True)
        stat_ref[i, 2:3, :] = jnp.sum(own * down, axis=0, keepdims=True)

    def crossing(keys, queries):
        seen = slice((blocks - keys) * BLOCK, rows)
        key_rows, value_rows = pk_ref[seen, column(g)], pv_ref[seen, column(g)]
        probs, dscores, query_rows, grad_rows = [], [], [], []
        for i in range(queries):
            query_rows.append(stacked(q_ref, i, g, heads))
            grad_rows.append(stacked(g_ref, i, g, heads))
            prev = dot(key_rows, query_rows[i], NT) * (SCALE * LOG2E)
            prev = masked(prev, start_ref[:, i * BLOCK : (i + 1) * BLOCK], -keys * BLOCK)
            own_top, own_total, own_sum = (stat_ref[i, n : n + 1, :] for n in range(3))
            top = jnp.maximum(own_top, jnp.max(prev, axis=0, keepdims=True))
            prev = jnp.exp2(prev - top)
            kept = jnp.exp2(own_top - top)
            dprev = dot(value_rows, grad_rows[i], NT)
            total = own_total * kept + jnp.sum(prev, axis=0, keepdims=True)
            dsum = own_sum * kept + jnp.sum(prev * dprev, axis=0, keepdims=True)
            stat_ref[i, 0:1, :] = top
            stat_ref[i, 1:2, :] = total
            stat_ref[i, 2:3, :] = dsum
            inverse = 1.0 / total
            prob = prev * inverse
            dscore = (prob * (dprev - dsum * inverse)).astype(jnp.bfloat16)
            probs.append(prob.astype(jnp.bfloat16))
            dscores.append(dscore)
        probs, dscores = (jnp.concatenate(x, axis=1) for x in (probs, dscores))
        query_rows, grad_rows = (jnp.concatenate(x, axis=0) for x in (query_rows, grad_rows))
        send_ref[seen, HEAD_WIDTH:] = dot(probs, grad_rows, NN).astype(jnp.bfloat16)
        send_ref[seen, :HEAD_WIDTH] = (dot(dscores, query_rows, NN) * SCALE).astype(jnp.bfloat16)
        dq = dot(key_rows, dscores, TN)
        for i in range(queries):
            dq_ref[i] = dq[:, i * heads * BLOCK : (i + 1) * heads * BLOCK]
        if keys < blocks:
            rest = slice(0, (blocks - keys) * BLOCK)
            send_ref[rest, :] = jnp.zeros(send_ref[rest, :].shape, jnp.bfloat16)

    for keys in range(1, blocks + 1):
        for queries in range(1, blocks + 2 - keys):
            pl.when((before == keys) & (after == queries))(
                functools.partial(crossing, keys, queries)
            )

    @pl.when(after == 0)
    def _():
        send_ref[...] = jnp.zeros(send_ref.shape, jnp.bfloat16)


def own_kernel(kv_heads, *refs):
    reach_ref, q_ref, g_ref, k_ref, v_ref, start_ref = refs[:6]
    per_head = [refs[6 + 2 * g : 8 + 2 * g] for g in range(kv_heads)]
    refs = refs[6 + 2 * kv_heads :]
    dq_hbm, keeps, (dq_ref, dk_ref, dv_ref, sems) = refs[0], refs[1 : 1 + kv_heads], refs[1 + kv_heads :]
    rows, width = q_ref.shape
    heads = width // k_ref.shape[1]
    blocks = rows // BLOCK
    reach = reach_ref[0]
    copies = []
    for g in range(kv_heads):
        stat_ref, dqp_ref = per_head[g]
        for i in reversed(range(blocks)):
            seen = slice(0, (i + 1) * BLOCK)
            query_rows, grad_rows, own, down = own_block(
                i, g, heads, q_ref, g_ref, k_ref, v_ref, start_ref
            )
            top, total, dsum = (stat_ref[i, n : n + 1, :] for n in range(3))
            inverse = 1.0 / total
            own = jnp.exp2(own - top) * inverse
            down = (own * (down - dsum * inverse)).astype(jnp.bfloat16)
            dv = dot(own.astype(jnp.bfloat16), grad_rows, NN)
            dk = dot(down, query_rows, NN)
            if i == blocks - 1:
                dv_ref[...] = dv
                dk_ref[...] = dk
            else:
                dv_ref[seen, :] += dv
                dk_ref[seen, :] += dk
            dq = dot(k_ref[seen, column(g)], down, TN)
            dq = (dq + jnp.where(i < reach, dqp_ref[i], 0.0)) * SCALE
            place = (
                pl.ds(i * BLOCK, BLOCK),
                pl.ds(g * heads * HEAD_WIDTH, heads * HEAD_WIDTH),
            )
            for h in range(heads):
                dq_ref[place[0], pl.ds((g * heads + h) * HEAD_WIDTH, HEAD_WIDTH)] = jnp.transpose(
                    dq[:, h * BLOCK : (h + 1) * BLOCK]
                ).astype(jnp.bfloat16)
            copy = pltpu.make_async_copy(
                dq_ref.at[place], dq_hbm.at[place], sems.at[g * blocks + i]
            )
            copy.start()
            copies.append(copy)
        keeps[g][:, :HEAD_WIDTH] = dk_ref[...] * SCALE
        keeps[g][:, HEAD_WIDTH:] = dv_ref[...]
    for copy in copies:
        copy.wait()


def sum_kernel(kv_heads, *refs):
    keep, back = refs[:kv_heads], refs[kv_heads : 2 * kv_heads]
    dk_ref, dv_ref = refs[2 * kv_heads :]
    for g in range(kv_heads):
        total = keep[g][...] + back[g][...].astype(jnp.float32)
        dk_ref[:, column(g)] = total[:, :HEAD_WIDTH].astype(jnp.bfloat16)
        dv_ref[:, column(g)] = total[:, HEAD_WIDTH:].astype(jnp.bfloat16)


def body(queries, keys, values, output_gradient, doc_lengths):
    rows = queries.shape[0]
    kv_heads = keys.shape[1] // HEAD_WIDTH
    heads = queries.shape[1] // keys.shape[1]
    blocks = rows // BLOCK
    lanes = heads * BLOCK
    axes = ("seq", "head")
    prev_keys = rotated(keys, "seq", 1)
    prev_values = rotated(values, "seq", 1)
    row = lengths_row(doc_lengths, axes)
    for group in round_groups():
        row = summed_round(row, axes, group)
    first = (lax.axis_index("seq") * rows).astype(jnp.int32).reshape(1)
    params = pltpu.CompilerParams(vmem_limit_bytes=24 * 1024 * 1024)
    shape = jax.ShapeDtypeStruct
    vmem = pl.BlockSpec(memory_space=pltpu.VMEM)
    smem = pl.BlockSpec(memory_space=pltpu.SMEM)
    hbm = pl.BlockSpec(memory_space=pltpu.HBM)
    pair = shape((rows, 2 * HEAD_WIDTH), jnp.bfloat16)
    per_head = [
        pair,
        shape((blocks, 8, lanes), jnp.float32),
        shape((blocks, HEAD_WIDTH, lanes), jnp.float32),
    ]
    arrays = (queries, output_gradient, keys, values)
    fetched = pl.pallas_call(
        functools.partial(fetch_kernel, len(arrays)),
        out_shape=[shape(a.shape, a.dtype) for a in arrays],
        in_specs=[hbm] * len(arrays),
        out_specs=[vmem] * len(arrays),
        scratch_shapes=[pltpu.SemaphoreType.DMA((2 * len(arrays),))],
        compiler_params=params,
        name="fetch",
    )(*(pltpu.with_memory_space_constraint(a, pltpu.HBM) for a in arrays))
    send, stat, dq, reach, start = pl.pallas_call(
        functools.partial(prev_kernel, 0),
        out_shape=per_head
        + [shape((1,), jnp.int32), shape((1, rows), jnp.int32)],
        in_specs=[smem] + [vmem] * 7,
        out_specs=[vmem] * 3 + [smem, vmem],
        compiler_params=params,
        name="prev_grads",
    )(first, row, prev_keys, prev_values, *fetched)
    sends, stats = [send], [stat, dq]
    for g in range(1, kv_heads):
        send, stat, dq = pl.pallas_call(
            functools.partial(prev_kernel, g),
            out_shape=per_head,
            in_specs=[smem] + [vmem] * 8,
            out_specs=[vmem] * 3,
            compiler_params=params,
            name="prev_grads",
        )(first, row, prev_keys, prev_values, *fetched, start)
        sends.append(send)
        stats += [stat, dq]
    backs = [rotated(send, "seq", -1) for send in sends]
    grad_queries, *keeps = pl.pallas_call(
        functools.partial(own_kernel, kv_heads),
        out_shape=[shape(queries.shape, jnp.bfloat16)]
        + [shape(pair.shape, jnp.float32)] * kv_heads,
        in_specs=[smem] + [vmem] * (5 + 2 * kv_heads),
        out_specs=[hbm] + [vmem] * kv_heads,
        scratch_shapes=[pltpu.VMEM(queries.shape, jnp.bfloat16)]
        + [pltpu.VMEM((rows, HEAD_WIDTH), jnp.float32)] * 2
        + [pltpu.SemaphoreType.DMA((kv_heads * blocks,))],
        compiler_params=params,
        name="own_grads",
    )(reach, *fetched, start, *stats)
    key_gradient, value_gradient = pl.pallas_call(
        functools.partial(sum_kernel, kv_heads),
        out_shape=[shape(keys.shape, jnp.bfloat16)] * 2,
        compiler_params=params,
        name="sums",
    )(*keeps, *backs)
    return (grad_queries, key_gradient, value_gradient)


def solution(mesh):
    in_specs = (
        P("seq", "head"),
        P("seq", "head"),
        P("seq", "head"),
        P("seq", "head"),
        P(("seq", "head")),
    )
    out_specs = (P("seq", "head"), P("seq", "head"), P("seq", "head"))
    return jax.shard_map(body, mesh=mesh, in_specs=in_specs, out_specs=out_specs, check_vma=False)
```

```python
import functools

import jax
import jax.numpy as jnp
from jax import lax
from jax.experimental import pallas as pl
from jax.experimental.pallas import tpu as pltpu
from jax.sharding import PartitionSpec as P

HEAD_WIDTH = 128
BLOCK = 128
SCALE = HEAD_WIDTH ** (-0.5)
LOG2E = 1.4426950408889634
NT = (((1,), (1,)), ((), ()))
NN = (((1,), (0,)), ((), ()))
TN = (((0,), (0,)), ((), ()))


def dot(a, b, dims):
    return lax.dot_general(a, b, dims, preferred_element_type=jnp.float32)


def rotated(value, axis, steps):
    count = lax.axis_size(axis)
    return lax.ppermute(value, axis, [(s, (s + steps) % count) for s in range(count)])


def round_groups():
    low = lax.axis_size("head")
    count = low * lax.axis_size("seq")
    bits = [1 << b for b in range(count.bit_length() - 1)]
    head, seq = [b for b in bits if b < low], [b for b in bits if b > low]
    return [[low]] + [part[n : n + 2] for part in (head, seq) for n in range(0, len(part), 2)]


def summed_round(value, axes, group):
    count = lax.axis_size(axes)
    masks = group + [sum(group)] * (len(group) - 1)
    others = [lax.ppermute(value, axes, [(s, s ^ m) for s in range(count)]) for m in masks]
    return functools.reduce(jnp.add, others, value)


def lengths_row(doc_lengths, axes):
    own = doc_lengths.shape[0]
    shards = lax.axis_size(axes)
    spot = lax.broadcasted_iota(jnp.int32, (1, shards, own), 1) == lax.axis_index(axes)
    return jnp.where(spot, doc_lengths[None, None, :], 0).reshape(1, shards * own)


def start_row(lengths, first, rows):
    docs = lengths.shape[1]
    before = lax.broadcasted_iota(jnp.int32, (docs, docs), 1) < lax.broadcasted_iota(
        jnp.int32, (docs, docs), 0
    )
    starts = jnp.sum(
        jnp.where(before, jnp.broadcast_to(lengths, (docs, docs)), 0), axis=1, keepdims=True
    )
    starts = jnp.broadcast_to(starts - first, (docs, rows))
    own = lax.broadcasted_iota(jnp.int32, (docs, rows), 1)
    return jnp.max(jnp.where(starts <= own, starts, -first), axis=0, keepdims=True)


def stacked(ref, i, g, heads):
    return jnp.concatenate(
        [
            ref[pl.ds(i * BLOCK, BLOCK), pl.ds((g * heads + h) * HEAD_WIDTH, HEAD_WIDTH)]
            for h in range(heads)
        ],
        axis=0,
    )


def masked(scores, start, first_key, query=None):
    key = first_key + lax.broadcasted_iota(jnp.int32, (scores.shape[0], BLOCK), 0)
    allowed = key >= start
    if query is not None:
        allowed = allowed & (key <= query)
    return jnp.concatenate(
        [
            jnp.where(allowed, scores[:, c : c + BLOCK], -jnp.inf)
            for c in range(0, scores.shape[1], BLOCK)
        ],
        axis=1,
    )


def column(g):
    return slice(g * HEAD_WIDTH, (g + 1) * HEAD_WIDTH)


def own_block(i, g, heads, q_ref, g_ref, k_ref, v_ref, start_ref):
    at, seen = slice(i * BLOCK, (i + 1) * BLOCK), slice(0, (i + 1) * BLOCK)
    query_rows, grad_rows = stacked(q_ref, i, g, heads), stacked(g_ref, i, g, heads)
    query = i * BLOCK + lax.broadcasted_iota(jnp.int32, (1, BLOCK), 1)
    scores = dot(k_ref[seen, column(g)], query_rows, NT) * (SCALE * LOG2E)
    scores = masked(scores, start_ref[:, at], 0, query)
    return query_rows, grad_rows, scores, dot(v_ref[seen, column(g)], grad_rows, NT)


def own_sums(stat_ref, i, g, heads, q_ref, g_ref, k_ref, v_ref, start_ref):
    _, _, own, down = own_block(i, g, heads, q_ref, g_ref, k_ref, v_ref, start_ref)
    top = jnp.max(own, axis=0, keepdims=True)
    own = jnp.exp2(own - top)
    stat_ref[0:1, :] = top
    stat_ref[1:2, :] = jnp.sum(own, axis=0, keepdims=True)
    stat_ref[2:3, :] = jnp.sum(own * down, axis=0, keepdims=True)


def fetch_kernel(count, after_ref, *refs):
    sources, targets, sems = refs[:count], refs[count : 2 * count], refs[2 * count]
    half = sources[0].shape[0] // 2
    copies = []
    for source, target in zip(sources, targets):
        for at in (pl.ds(0, half), pl.ds(half, half)):
            copies.append(
                pltpu.make_async_copy(source.at[at], target.at[at], sems.at[len(copies)])
            )
            copies[-1].start()
    for copy in copies:
        copy.wait()


def first_kernel(first_ref, len_ref, q_ref, g_ref, k_ref, v_ref, stat_ref, start_ref):
    rows, width = q_ref.shape

    @pl.when(first_ref[0] == 0)
    def _():
        start_ref[...] = start_row(len_ref[...], first_ref[0], rows)
        for g in range(k_ref.shape[1] // HEAD_WIDTH):
            for i in range(rows // BLOCK):
                own_sums(
                    stat_ref.at[g, i], i, g, width // k_ref.shape[1],
                    q_ref, g_ref, k_ref, v_ref, start_ref,
                )


def prev_kernel(g, first_ref, len_ref, pk_ref, pv_ref, *refs):
    q_ref, g_ref, k_ref, v_ref = refs[:4]
    if g == 0:
        send_ref, stat_ref, dq_ref, reach_ref, start_ref = refs[5:]
    else:
        start_ref, send_ref, stat_ref, dq_ref = refs[4:]
    rows, width = q_ref.shape
    heads = width // k_ref.shape[1]
    blocks = rows // BLOCK
    if g == 0:
        start_ref[...] = start_row(len_ref[...], first_ref[0], rows)
    start = start_ref[...]
    after = pl.cdiv(jnp.sum((start < 0).astype(jnp.int32)), BLOCK)
    if g == 0:
        reach_ref[0] = after
    def crossing(keys, queries):
        seen = slice((blocks - keys) * BLOCK, rows)
        key_rows, value_rows = pk_ref[seen, column(g)], pv_ref[seen, column(g)]
        probs, dscores, query_rows, grad_rows = [], [], [], []
        for i in range(queries):
            rows_i, grads_i, own, down = own_block(
                i, g, heads, q_ref, g_ref, k_ref, v_ref, start_ref
            )
            query_rows.append(rows_i)
            grad_rows.append(grads_i)
            prev = dot(key_rows, rows_i, NT) * (SCALE * LOG2E)
            prev = masked(prev, start_ref[:, i * BLOCK : (i + 1) * BLOCK], -keys * BLOCK)
            dprev = dot(value_rows, grads_i, NT)
            top = jnp.maximum(
                jnp.max(own, axis=0, keepdims=True), jnp.max(prev, axis=0, keepdims=True)
            )
            own, prev = jnp.exp2(own - top), jnp.exp2(prev - top)
            total = jnp.sum(own, axis=0, keepdims=True) + jnp.sum(prev, axis=0, keepdims=True)
            dsum = jnp.sum(own * down, axis=0, keepdims=True) + jnp.sum(
                prev * dprev, axis=0, keepdims=True
            )
            stat_ref[i, 0:1, :] = top
            stat_ref[i, 1:2, :] = total
            stat_ref[i, 2:3, :] = dsum
            inverse = 1.0 / total
            prob = prev * inverse
            dscore = (prob * (dprev - dsum * inverse)).astype(jnp.bfloat16)
            probs.append(prob.astype(jnp.bfloat16))
            dscores.append(dscore)
        probs, dscores = (jnp.concatenate(x, axis=1) for x in (probs, dscores))
        query_rows, grad_rows = (jnp.concatenate(x, axis=0) for x in (query_rows, grad_rows))
        send_ref[seen, HEAD_WIDTH:] = dot(probs, grad_rows, NN).astype(jnp.bfloat16)
        send_ref[seen, :HEAD_WIDTH] = (dot(dscores, query_rows, NN) * SCALE).astype(jnp.bfloat16)
        dq = dot(key_rows, dscores, TN)
        for i in range(queries):
            dq_ref[i] = dq[:, i * heads * BLOCK : (i + 1) * heads * BLOCK]
        if keys < blocks:
            rest = slice(0, (blocks - keys) * BLOCK)
            send_ref[rest, :] = jnp.zeros(send_ref[rest, :].shape, jnp.bfloat16)

    for queries in range(1, blocks + 1):
        pl.when(after == queries)(functools.partial(crossing, blocks + 1 - queries, queries))

    @pl.when(after == 0)
    def _():
        send_ref[...] = jnp.zeros(send_ref.shape, jnp.bfloat16)


def own_kernel(kv_heads, *refs):
    first_ref, reach_ref, q_ref, g_ref, k_ref, v_ref, start_ref, stat_ref = refs[:8]
    per_head = [refs[8 + 2 * g : 10 + 2 * g] for g in range(kv_heads)]
    refs = refs[8 + 2 * kv_heads :]
    dq_hbm, keeps, (dq_ref, dk_ref, dv_ref, sums_ref, sems) = refs[0], refs[1 : 1 + kv_heads], refs[1 + kv_heads :]
    rows, width = q_ref.shape
    heads = width // k_ref.shape[1]
    blocks = rows // BLOCK
    reach = reach_ref[0]
    @pl.when(first_ref[0] == 0)
    def _():
        sums_ref[...] = stat_ref[...]

    for g in range(kv_heads):
        for i in range(blocks):

            @pl.when(i < reach)
            def _():
                sums_ref[g, i] = per_head[g][0][i]

            @pl.when((first_ref[0] > 0) & (i >= reach))
            def _():
                own_sums(sums_ref.at[g, i], i, g, heads, q_ref, g_ref, k_ref, v_ref, start_ref)

    copies = []
    for g in range(kv_heads):
        dqp_ref = per_head[g][1]
        for i in reversed(range(blocks)):
            seen = slice(0, (i + 1) * BLOCK)
            query_rows, grad_rows, own, down = own_block(
                i, g, heads, q_ref, g_ref, k_ref, v_ref, start_ref
            )
            top, total, dsum = (sums_ref[g, i, n : n + 1, :] for n in range(3))
            inverse = 1.0 / total
            own = jnp.exp2(own - top) * inverse
            down = (own * (down - dsum * inverse)).astype(jnp.bfloat16)
            dv = dot(own.astype(jnp.bfloat16), grad_rows, NN)
            dk = dot(down, query_rows, NN)
            if i == blocks - 1:
                dv_ref[...] = dv
                dk_ref[...] = dk
            else:
                dv_ref[seen, :] += dv
                dk_ref[seen, :] += dk
            dq = dot(k_ref[seen, column(g)], down, TN)
            dq = (dq + jnp.where(i < reach, dqp_ref[i], 0.0)) * SCALE
            place = (
                pl.ds(i * BLOCK, BLOCK),
                pl.ds(g * heads * HEAD_WIDTH, heads * HEAD_WIDTH),
            )
            for h in range(heads):
                dq_ref[place[0], pl.ds((g * heads + h) * HEAD_WIDTH, HEAD_WIDTH)] = jnp.transpose(
                    dq[:, h * BLOCK : (h + 1) * BLOCK]
                ).astype(jnp.bfloat16)
            copy = pltpu.make_async_copy(
                dq_ref.at[place], dq_hbm.at[place], sems.at[g * blocks + i]
            )
            copy.start()
            copies.append(copy)
        keeps[g][:, :HEAD_WIDTH] = dk_ref[...] * SCALE
        keeps[g][:, HEAD_WIDTH:] = dv_ref[...]
    for copy in copies:
        copy.wait()


def sum_kernel(kv_heads, *refs):
    keep, back = refs[:kv_heads], refs[kv_heads : 2 * kv_heads]
    dk_ref, dv_ref = refs[2 * kv_heads :]
    for g in range(kv_heads):
        total = keep[g][...] + back[g][...].astype(jnp.float32)
        dk_ref[:, column(g)] = total[:, :HEAD_WIDTH].astype(jnp.bfloat16)
        dv_ref[:, column(g)] = total[:, HEAD_WIDTH:].astype(jnp.bfloat16)


def body(queries, keys, values, output_gradient, doc_lengths):
    rows = queries.shape[0]
    kv_heads = keys.shape[1] // HEAD_WIDTH
    heads = queries.shape[1] // keys.shape[1]
    blocks = rows // BLOCK
    lanes = heads * BLOCK
    axes = ("seq", "head")
    prev_keys = rotated(keys, "seq", 1)
    prev_values = rotated(values, "seq", 1)
    row = lengths_row(doc_lengths, axes)
    known = []
    for group in round_groups():
        row = summed_round(row, axes, group)
        known.append(row)
    first = (lax.axis_index("seq") * rows).astype(jnp.int32).reshape(1)
    params = pltpu.CompilerParams(vmem_limit_bytes=24 * 1024 * 1024)
    shape = jax.ShapeDtypeStruct
    vmem = pl.BlockSpec(memory_space=pltpu.VMEM)
    smem = pl.BlockSpec(memory_space=pltpu.SMEM)
    hbm = pl.BlockSpec(memory_space=pltpu.HBM)
    pair = shape((rows, 2 * HEAD_WIDTH), jnp.bfloat16)
    per_head = [
        pair,
        shape((blocks, 8, lanes), jnp.float32),
        shape((blocks, HEAD_WIDTH, lanes), jnp.float32),
    ]
    arrays = (queries, output_gradient, keys, values)
    fetched = pl.pallas_call(
        functools.partial(fetch_kernel, len(arrays)),
        out_shape=[shape(a.shape, a.dtype) for a in arrays],
        in_specs=[hbm] * (1 + len(arrays)),
        out_specs=[vmem] * len(arrays),
        scratch_shapes=[pltpu.SemaphoreType.DMA((2 * len(arrays),))],
        compiler_params=params,
        name="fetch",
    )(known[1], *(pltpu.with_memory_space_constraint(a, pltpu.HBM) for a in arrays))
    first_stats = pl.pallas_call(
        first_kernel,
        out_shape=shape((kv_heads, blocks, 8, lanes), jnp.float32),
        in_specs=[smem] + [vmem] * 5,
        out_specs=vmem,
        scratch_shapes=[pltpu.VMEM((1, rows), jnp.int32)],
        compiler_params=params,
        name="first_sums",
    )(first, row, *fetched)
    send, stat, dq, reach, start = pl.pallas_call(
        functools.partial(prev_kernel, 0),
        out_shape=per_head
        + [shape((1,), jnp.int32), shape((1, rows), jnp.int32)],
        in_specs=[smem] + [vmem] * 8,
        out_specs=[vmem] * 3 + [smem, vmem],
        compiler_params=params,
        name="prev_grads",
    )(first, row, prev_keys, prev_values, *fetched, first_stats)
    sends, stats = [send], [stat, dq]
    for g in range(1, kv_heads):
        send, stat, dq = pl.pallas_call(
            functools.partial(prev_kernel, g),
            out_shape=per_head,
            in_specs=[smem] + [vmem] * 8,
            out_specs=[vmem] * 3,
            compiler_params=params,
            name="prev_grads",
        )(first, row, prev_keys, prev_values, *fetched, start)
        sends.append(send)
        stats += [stat, dq]
    backs = [rotated(send, "seq", -1) for send in sends]
    grad_queries, *keeps = pl.pallas_call(
        functools.partial(own_kernel, kv_heads),
        out_shape=[shape(queries.shape, jnp.bfloat16)]
        + [shape(pair.shape, jnp.float32)] * kv_heads,
        in_specs=[smem] * 2 + [vmem] * (6 + 2 * kv_heads),
        out_specs=[hbm] + [vmem] * kv_heads,
        scratch_shapes=[pltpu.VMEM(queries.shape, jnp.bfloat16)]
        + [pltpu.VMEM((rows, HEAD_WIDTH), jnp.float32)] * 2
        + [pltpu.VMEM((kv_heads, blocks, 8, lanes), jnp.float32)]
        + [pltpu.SemaphoreType.DMA((kv_heads * blocks,))],
        compiler_params=params,
        name="own_grads",
    )(first, reach, *fetched, start, first_stats, *stats)
    key_gradient, value_gradient = pl.pallas_call(
        functools.partial(sum_kernel, kv_heads),
        out_shape=[shape(keys.shape, jnp.bfloat16)] * 2,
        compiler_params=params,
        name="sums",
    )(*keeps, *backs)
    return (grad_queries, key_gradient, value_gradient)


def solution(mesh):
    in_specs = (
        P("seq", "head"),
        P("seq", "head"),
        P("seq", "head"),
        P("seq", "head"),
        P(("seq", "head")),
    )
    out_specs = (P("seq", "head"), P("seq", "head"), P("seq", "head"))
    return jax.shard_map(body, mesh=mesh, in_specs=in_specs, out_specs=out_specs, check_vma=False)
```

```python
import functools

import jax
import jax.numpy as jnp
from jax import lax
from jax.experimental import pallas as pl
from jax.experimental.pallas import tpu as pltpu
from jax.sharding import PartitionSpec as P

HEAD_WIDTH = 128
BLOCK = 128
SCALE = HEAD_WIDTH ** (-0.5)
LOG2E = 1.4426950408889634
NT = (((1,), (1,)), ((), ()))
NN = (((1,), (0,)), ((), ()))
TN = (((0,), (0,)), ((), ()))


def dot(a, b, dims):
    return lax.dot_general(a, b, dims, preferred_element_type=jnp.float32)


def rotated(value, axis, steps):
    count = lax.axis_size(axis)
    return lax.ppermute(value, axis, [(s, (s + steps) % count) for s in range(count)])


def round_groups():
    low = lax.axis_size("head")
    count = low * lax.axis_size("seq")
    bits = [1 << b for b in range(count.bit_length() - 1)]
    head, seq = [b for b in bits if b < low], [b for b in bits if b > low]
    return [part[n : n + 2] for part in (head, seq) for n in range(0, len(part), 2)]


def summed_round(value, axes, group):
    count = lax.axis_size(axes)
    masks = group + [sum(group)] * (len(group) - 1)
    others = [lax.ppermute(value, axes, [(s, s ^ m) for s in range(count)]) for m in masks]
    return functools.reduce(jnp.add, others, value)


def lengths_row(doc_lengths, place, shards):
    own = doc_lengths.shape[0]
    spot = lax.broadcasted_iota(jnp.int32, (1, shards, own), 1) == place
    return jnp.where(spot, doc_lengths[None, None, :], 0).reshape(1, shards * own)


def start_row(lengths, first, rows):
    docs = lengths.shape[1]
    before = lax.broadcasted_iota(jnp.int32, (docs, docs), 1) < lax.broadcasted_iota(
        jnp.int32, (docs, docs), 0
    )
    starts = jnp.sum(
        jnp.where(before, jnp.broadcast_to(lengths, (docs, docs)), 0), axis=1, keepdims=True
    )
    starts = jnp.broadcast_to(starts - first, (docs, rows))
    own = lax.broadcasted_iota(jnp.int32, (docs, rows), 1)
    return jnp.max(jnp.where(starts <= own, starts, -first), axis=0, keepdims=True)


def stacked(ref, i, g, heads):
    return jnp.concatenate(
        [
            ref[pl.ds(i * BLOCK, BLOCK), pl.ds((g * heads + h) * HEAD_WIDTH, HEAD_WIDTH)]
            for h in range(heads)
        ],
        axis=0,
    )


def masked(scores, start, first_key, query=None):
    key = first_key + lax.broadcasted_iota(jnp.int32, (scores.shape[0], BLOCK), 0)
    allowed = key >= start
    if query is not None:
        allowed = allowed & (key <= query)
    return jnp.concatenate(
        [
            jnp.where(allowed, scores[:, c : c + BLOCK], -jnp.inf)
            for c in range(0, scores.shape[1], BLOCK)
        ],
        axis=1,
    )


def column(g):
    return slice(g * HEAD_WIDTH, (g + 1) * HEAD_WIDTH)


def own_block(i, g, heads, q_ref, g_ref, k_ref, v_ref, start_ref):
    at, seen = slice(i * BLOCK, (i + 1) * BLOCK), slice(0, (i + 1) * BLOCK)
    query_rows, grad_rows = stacked(q_ref, i, g, heads), stacked(g_ref, i, g, heads)
    query = i * BLOCK + lax.broadcasted_iota(jnp.int32, (1, BLOCK), 1)
    scores = dot(k_ref[seen, column(g)], query_rows, NT) * (SCALE * LOG2E)
    scores = masked(scores, start_ref[:, at], 0, query)
    return query_rows, grad_rows, scores, dot(v_ref[seen, column(g)], grad_rows, NT)


def own_sums(stat_ref, i, g, heads, q_ref, g_ref, k_ref, v_ref, start_ref):
    _, _, own, down = own_block(i, g, heads, q_ref, g_ref, k_ref, v_ref, start_ref)
    top = jnp.max(own, axis=0, keepdims=True)
    own = jnp.exp2(own - top)
    stat_ref[0:1, :] = top
    stat_ref[1:2, :] = jnp.sum(own, axis=0, keepdims=True)
    stat_ref[2:3, :] = jnp.sum(own * down, axis=0, keepdims=True)


def fetch_kernel(count, after_ref, *refs):
    sources, targets, sems = refs[:count], refs[count : 2 * count], refs[2 * count]
    half = sources[0].shape[0] // 2
    copies = []
    for source, target in zip(sources, targets):
        for at in (pl.ds(0, half), pl.ds(half, half)):
            copies.append(
                pltpu.make_async_copy(source.at[at], target.at[at], sems.at[len(copies)])
            )
            copies[-1].start()
    for copy in copies:
        copy.wait()


def first_kernel(first_ref, len_ref, q_ref, g_ref, k_ref, v_ref, stat_ref, start_ref):
    rows, width = q_ref.shape

    @pl.when(first_ref[0] == 0)
    def _():
        start_ref[...] = start_row(len_ref[...], first_ref[0], rows)
        for g in range(k_ref.shape[1] // HEAD_WIDTH):
            for i in range(rows // BLOCK):
                own_sums(
                    stat_ref.at[g, i], i, g, width // k_ref.shape[1],
                    q_ref, g_ref, k_ref, v_ref, start_ref,
                )


def prev_kernel(g, first_ref, len_ref, pk_ref, pv_ref, *refs):
    q_ref, g_ref, k_ref, v_ref = refs[:4]
    if g == 0:
        send_ref, stat_ref, dq_ref, reach_ref, start_ref = refs[5:]
    else:
        start_ref, send_ref, stat_ref, dq_ref = refs[4:]
    rows, width = q_ref.shape
    heads = width // k_ref.shape[1]
    blocks = rows // BLOCK
    if g == 0:
        start_ref[...] = start_row(len_ref[...], first_ref[0], rows)
    start = start_ref[...]
    after = pl.cdiv(jnp.sum((start < 0).astype(jnp.int32)), BLOCK)
    if g == 0:
        reach_ref[0] = after
    def crossing(keys, queries):
        seen = slice((blocks - keys) * BLOCK, rows)
        key_rows, value_rows = pk_ref[seen, column(g)], pv_ref[seen, column(g)]
        probs, dscores, query_rows, grad_rows = [], [], [], []
        for i in range(queries):
            rows_i, grads_i, own, down = own_block(
                i, g, heads, q_ref, g_ref, k_ref, v_ref, start_ref
            )
            query_rows.append(rows_i)
            grad_rows.append(grads_i)
            prev = dot(key_rows, rows_i, NT) * (SCALE * LOG2E)
            prev = masked(prev, start_ref[:, i * BLOCK : (i + 1) * BLOCK], -keys * BLOCK)
            dprev = dot(value_rows, grads_i, NT)
            top = jnp.maximum(
                jnp.max(own, axis=0, keepdims=True), jnp.max(prev, axis=0, keepdims=True)
            )
            own, prev = jnp.exp2(own - top), jnp.exp2(prev - top)
            total = jnp.sum(own, axis=0, keepdims=True) + jnp.sum(prev, axis=0, keepdims=True)
            dsum = jnp.sum(own * down, axis=0, keepdims=True) + jnp.sum(
                prev * dprev, axis=0, keepdims=True
            )
            stat_ref[i, 0:1, :] = top
            stat_ref[i, 1:2, :] = total
            stat_ref[i, 2:3, :] = dsum
            inverse = 1.0 / total
            prob = prev * inverse
            dscore = (prob * (dprev - dsum * inverse)).astype(jnp.bfloat16)
            probs.append(prob.astype(jnp.bfloat16))
            dscores.append(dscore)
        probs, dscores = (jnp.concatenate(x, axis=1) for x in (probs, dscores))
        query_rows, grad_rows = (jnp.concatenate(x, axis=0) for x in (query_rows, grad_rows))
        send_ref[seen, HEAD_WIDTH:] = dot(probs, grad_rows, NN).astype(jnp.bfloat16)
        send_ref[seen, :HEAD_WIDTH] = (dot(dscores, query_rows, NN) * SCALE).astype(jnp.bfloat16)
        dq = dot(key_rows, dscores, TN)
        for i in range(queries):
            dq_ref[i] = dq[:, i * heads * BLOCK : (i + 1) * heads * BLOCK]
        if keys < blocks:
            rest = slice(0, (blocks - keys) * BLOCK)
            send_ref[rest, :] = jnp.zeros(send_ref[rest, :].shape, jnp.bfloat16)

    for queries in range(1, blocks + 1):
        pl.when(after == queries)(functools.partial(crossing, blocks + 1 - queries, queries))

    @pl.when(after == 0)
    def _():
        send_ref[...] = jnp.zeros(send_ref.shape, jnp.bfloat16)


def own_kernel(kv_heads, *refs):
    first_ref, reach_ref, q_ref, g_ref, k_ref, v_ref, start_ref, stat_ref = refs[:8]
    per_head = [refs[8 + 2 * g : 10 + 2 * g] for g in range(kv_heads)]
    refs = refs[8 + 2 * kv_heads :]
    dq_hbm, keeps, (dq_ref, dk_ref, dv_ref, sums_ref, sems) = refs[0], refs[1 : 1 + kv_heads], refs[1 + kv_heads :]
    rows, width = q_ref.shape
    heads = width // k_ref.shape[1]
    blocks = rows // BLOCK
    reach = reach_ref[0]
    @pl.when(first_ref[0] == 0)
    def _():
        sums_ref[...] = stat_ref[...]

    for g in range(kv_heads):
        for i in range(blocks):

            @pl.when(i < reach)
            def _():
                sums_ref[g, i] = per_head[g][0][i]

            @pl.when((first_ref[0] > 0) & (i >= reach))
            def _():
                own_sums(sums_ref.at[g, i], i, g, heads, q_ref, g_ref, k_ref, v_ref, start_ref)

    copies = []
    for g in range(kv_heads):
        dqp_ref = per_head[g][1]
        for i in reversed(range(blocks)):
            seen = slice(0, (i + 1) * BLOCK)
            query_rows, grad_rows, own, down = own_block(
                i, g, heads, q_ref, g_ref, k_ref, v_ref, start_ref
            )
            top, total, dsum = (sums_ref[g, i, n : n + 1, :] for n in range(3))
            inverse = 1.0 / total
            own = jnp.exp2(own - top) * inverse
            down = (own * (down - dsum * inverse)).astype(jnp.bfloat16)
            dv = dot(own.astype(jnp.bfloat16), grad_rows, NN)
            dk = dot(down, query_rows, NN)
            if i == blocks - 1:
                dv_ref[...] = dv
                dk_ref[...] = dk
            else:
                dv_ref[seen, :] += dv
                dk_ref[seen, :] += dk
            dq = dot(k_ref[seen, column(g)], down, TN)
            dq = (dq + jnp.where(i < reach, dqp_ref[i], 0.0)) * SCALE
            place = (
                pl.ds(i * BLOCK, BLOCK),
                pl.ds(g * heads * HEAD_WIDTH, heads * HEAD_WIDTH),
            )
            for h in range(heads):
                dq_ref[place[0], pl.ds((g * heads + h) * HEAD_WIDTH, HEAD_WIDTH)] = jnp.transpose(
                    dq[:, h * BLOCK : (h + 1) * BLOCK]
                ).astype(jnp.bfloat16)
            copy = pltpu.make_async_copy(
                dq_ref.at[place], dq_hbm.at[place], sems.at[g * blocks + i]
            )
            copy.start()
            copies.append(copy)
        keeps[g][:, :HEAD_WIDTH] = dk_ref[...] * SCALE
        keeps[g][:, HEAD_WIDTH:] = dv_ref[...]
    for copy in copies:
        copy.wait()


def sum_kernel(kv_heads, *refs):
    keep, back = refs[:kv_heads], refs[kv_heads : 2 * kv_heads]
    dk_ref, dv_ref = refs[2 * kv_heads :]
    for g in range(kv_heads):
        total = keep[g][...] + back[g][...].astype(jnp.float32)
        dk_ref[:, column(g)] = total[:, :HEAD_WIDTH].astype(jnp.bfloat16)
        dv_ref[:, column(g)] = total[:, HEAD_WIDTH:].astype(jnp.bfloat16)


def body(queries, keys, values, output_gradient, doc_lengths):
    rows = queries.shape[0]
    kv_heads = keys.shape[1] // HEAD_WIDTH
    heads = queries.shape[1] // keys.shape[1]
    blocks = rows // BLOCK
    lanes = heads * BLOCK
    axes = ("seq", "head")
    prev_keys = rotated(keys, "seq", 1)
    prev_values = rotated(values, "seq", 1)
    shards, place, low = lax.axis_size(axes), lax.axis_index(axes), lax.axis_size("head")
    others = lax.ppermute(doc_lengths, axes, [(s, s ^ low) for s in range(shards)])
    row = lengths_row(doc_lengths, place, shards) + lengths_row(others, place ^ low, shards)
    row = lax.optimization_barrier(row)
    known = [row]
    for group in round_groups():
        row = summed_round(row, axes, group)
        known.append(row)
    first = (lax.axis_index("seq") * rows).astype(jnp.int32).reshape(1)
    params = pltpu.CompilerParams(vmem_limit_bytes=24 * 1024 * 1024)
    shape = jax.ShapeDtypeStruct
    vmem = pl.BlockSpec(memory_space=pltpu.VMEM)
    smem = pl.BlockSpec(memory_space=pltpu.SMEM)
    hbm = pl.BlockSpec(memory_space=pltpu.HBM)
    pair = shape((rows, 2 * HEAD_WIDTH), jnp.bfloat16)
    per_head = [
        pair,
        shape((blocks, 8, lanes), jnp.float32),
        shape((blocks, HEAD_WIDTH, lanes), jnp.float32),
    ]
    arrays = (queries, output_gradient, keys, values)
    fetched = pl.pallas_call(
        functools.partial(fetch_kernel, len(arrays)),
        out_shape=[shape(a.shape, a.dtype) for a in arrays],
        in_specs=[hbm] * (1 + len(arrays)),
        out_specs=[vmem] * len(arrays),
        scratch_shapes=[pltpu.SemaphoreType.DMA((2 * len(arrays),))],
        compiler_params=params,
        name="fetch",
    )(known[1], *(pltpu.with_memory_space_constraint(a, pltpu.HBM) for a in arrays))
    first_stats = pl.pallas_call(
        first_kernel,
        out_shape=shape((kv_heads, blocks, 8, lanes), jnp.float32),
        in_specs=[smem] + [vmem] * 5,
        out_specs=vmem,
        scratch_shapes=[pltpu.VMEM((1, rows), jnp.int32)],
        compiler_params=params,
        name="first_sums",
    )(first, row, *fetched)
    send, stat, dq, reach, start = pl.pallas_call(
        functools.partial(prev_kernel, 0),
        out_shape=per_head
        + [shape((1,), jnp.int32), shape((1, rows), jnp.int32)],
        in_specs=[smem] + [vmem] * 8,
        out_specs=[vmem] * 3 + [smem, vmem],
        compiler_params=params,
        name="prev_grads",
    )(first, row, prev_keys, prev_values, *fetched, first_stats)
    sends, stats = [send], [stat, dq]
    for g in range(1, kv_heads):
        send, stat, dq = pl.pallas_call(
            functools.partial(prev_kernel, g),
            out_shape=per_head,
            in_specs=[smem] + [vmem] * 8,
            out_specs=[vmem] * 3,
            compiler_params=params,
            name="prev_grads",
        )(first, row, prev_keys, prev_values, *fetched, start)
        sends.append(send)
        stats += [stat, dq]
    backs = [rotated(send, "seq", -1) for send in sends]
    grad_queries, *keeps = pl.pallas_call(
        functools.partial(own_kernel, kv_heads),
        out_shape=[shape(queries.shape, jnp.bfloat16)]
        + [shape(pair.shape, jnp.float32)] * kv_heads,
        in_specs=[smem] * 2 + [vmem] * (6 + 2 * kv_heads),
        out_specs=[hbm] + [vmem] * kv_heads,
        scratch_shapes=[pltpu.VMEM(queries.shape, jnp.bfloat16)]
        + [pltpu.VMEM((rows, HEAD_WIDTH), jnp.float32)] * 2
        + [pltpu.VMEM((kv_heads, blocks, 8, lanes), jnp.float32)]
        + [pltpu.SemaphoreType.DMA((kv_heads * blocks,))],
        compiler_params=params,
        name="own_grads",
    )(first, reach, *fetched, start, first_stats, *stats)
    key_gradient, value_gradient = pl.pallas_call(
        functools.partial(sum_kernel, kv_heads),
        out_shape=[shape(keys.shape, jnp.bfloat16)] * 2,
        compiler_params=params,
        name="sums",
    )(*keeps, *backs)
    return (grad_queries, key_gradient, value_gradient)


def solution(mesh):
    in_specs = (
        P("seq", "head"),
        P("seq", "head"),
        P("seq", "head"),
        P("seq", "head"),
        P(("seq", "head")),
    )
    out_specs = (P("seq", "head"), P("seq", "head"), P("seq", "head"))
    return jax.shard_map(body, mesh=mesh, in_specs=in_specs, out_specs=out_specs, check_vma=False)
```

```python
import functools

import jax
import jax.numpy as jnp
from jax import lax
from jax.experimental import pallas as pl
from jax.experimental.pallas import tpu as pltpu
from jax.sharding import PartitionSpec as P

HEAD_WIDTH = 128
BLOCK = 128
SCALE = HEAD_WIDTH ** (-0.5)
LOG2E = 1.4426950408889634
NT = (((1,), (1,)), ((), ()))
NN = (((1,), (0,)), ((), ()))
TN = (((0,), (0,)), ((), ()))


def dot(a, b, dims):
    return lax.dot_general(a, b, dims, preferred_element_type=jnp.float32)


def rotated(value, axis, steps):
    count = lax.axis_size(axis)
    return lax.ppermute(value, axis, [(s, (s + steps) % count) for s in range(count)])


def round_groups():
    low = lax.axis_size("head")
    count = low * lax.axis_size("seq")
    bits = [1 << b for b in range(count.bit_length() - 1)]
    head, seq = [b for b in bits if b < low], [b for b in bits if b > low]
    return [[low]] + [part[n : n + 2] for part in (head, seq) for n in range(0, len(part), 2)]


def summed_round(value, axes, group):
    count = lax.axis_size(axes)
    masks = group + [sum(group)] * (len(group) - 1)
    others = [lax.ppermute(value, axes, [(s, s ^ m) for s in range(count)]) for m in masks]
    return functools.reduce(jnp.add, others, value)


def lengths_row(doc_lengths, axes):
    own = doc_lengths.shape[0]
    shards = lax.axis_size(axes)
    spot = lax.broadcasted_iota(jnp.int32, (1, shards, own), 1) == lax.axis_index(axes)
    return jnp.where(spot, doc_lengths[None, None, :], 0).reshape(1, shards * own)


def start_row(lengths, first, rows):
    docs = lengths.shape[1]
    before = lax.broadcasted_iota(jnp.int32, (docs, docs), 1) < lax.broadcasted_iota(
        jnp.int32, (docs, docs), 0
    )
    starts = jnp.sum(
        jnp.where(before, jnp.broadcast_to(lengths, (docs, docs)), 0), axis=1, keepdims=True
    )
    starts = jnp.broadcast_to(starts - first, (docs, rows))
    own = lax.broadcasted_iota(jnp.int32, (docs, rows), 1)
    return jnp.max(jnp.where(starts <= own, starts, -first), axis=0, keepdims=True)


def stacked(ref, i, g, heads):
    return jnp.concatenate(
        [
            ref[pl.ds(i * BLOCK, BLOCK), pl.ds((g * heads + h) * HEAD_WIDTH, HEAD_WIDTH)]
            for h in range(heads)
        ],
        axis=0,
    )


def masked(scores, start, first_key, query=None):
    key = first_key + lax.broadcasted_iota(jnp.int32, (scores.shape[0], BLOCK), 0)
    allowed = key >= start
    if query is not None:
        allowed = allowed & (key <= query)
    return jnp.concatenate(
        [
            jnp.where(allowed, scores[:, c : c + BLOCK], -jnp.inf)
            for c in range(0, scores.shape[1], BLOCK)
        ],
        axis=1,
    )


def column(g):
    return slice(g * HEAD_WIDTH, (g + 1) * HEAD_WIDTH)


def own_block(i, g, heads, q_ref, g_ref, k_ref, v_ref, start_ref):
    at, seen = slice(i * BLOCK, (i + 1) * BLOCK), slice(0, (i + 1) * BLOCK)
    query_rows, grad_rows = stacked(q_ref, i, g, heads), stacked(g_ref, i, g, heads)
    query = i * BLOCK + lax.broadcasted_iota(jnp.int32, (1, BLOCK), 1)
    scores = dot(k_ref[seen, column(g)], query_rows, NT) * (SCALE * LOG2E)
    scores = masked(scores, start_ref[:, at], 0, query)
    return query_rows, grad_rows, scores, dot(v_ref[seen, column(g)], grad_rows, NT)


def own_sums(stat_ref, i, g, heads, q_ref, g_ref, k_ref, v_ref, start_ref):
    _, _, own, down = own_block(i, g, heads, q_ref, g_ref, k_ref, v_ref, start_ref)
    top = jnp.max(own, axis=0, keepdims=True)
    own = jnp.exp2(own - top)
    stat_ref[0:1, :] = top
    stat_ref[1:2, :] = jnp.sum(own, axis=0, keepdims=True)
    stat_ref[2:3, :] = jnp.sum(own * down, axis=0, keepdims=True)


def fetch_kernel(count, after_ref, *refs):
    sources, targets, sems = refs[:count], refs[count : 2 * count], refs[2 * count]
    half = sources[0].shape[0] // 2
    copies = []
    for source, target in zip(sources, targets):
        for at in (pl.ds(0, half), pl.ds(half, half)):
            copies.append(
                pltpu.make_async_copy(source.at[at], target.at[at], sems.at[len(copies)])
            )
            copies[-1].start()
    for copy in copies:
        copy.wait()


def first_kernel(first_ref, len_ref, q_ref, g_ref, k_ref, v_ref, stat_ref, start_ref):
    rows, width = q_ref.shape

    @pl.when(first_ref[0] == 0)
    def _():
        start_ref[...] = start_row(len_ref[...], first_ref[0], rows)
        for g in range(k_ref.shape[1] // HEAD_WIDTH):
            for i in range(rows // BLOCK):
                own_sums(
                    stat_ref.at[g, i], i, g, width // k_ref.shape[1],
                    q_ref, g_ref, k_ref, v_ref, start_ref,
                )


def prev_kernel(g, first_ref, len_ref, pk_ref, pv_ref, *refs):
    q_ref, g_ref, k_ref, v_ref = refs[:4]
    if g == 0:
        send_ref, stat_ref, dq_ref, reach_ref, start_ref = refs[5:]
    else:
        start_ref, send_ref, stat_ref, dq_ref = refs[4:]
    rows, width = q_ref.shape
    heads = width // k_ref.shape[1]
    blocks = rows // BLOCK
    if g == 0:
        start_ref[...] = start_row(len_ref[...], first_ref[0], rows)
    start = start_ref[...]
    after = pl.cdiv(jnp.sum((start < 0).astype(jnp.int32)), BLOCK)
    if g == 0:
        reach_ref[0] = after
    def crossing(keys, queries):
        seen = slice((blocks - keys) * BLOCK, rows)
        key_rows, value_rows = pk_ref[seen, column(g)], pv_ref[seen, column(g)]
        probs, dscores, query_rows, grad_rows = [], [], [], []
        for i in range(queries):
            rows_i, grads_i, own, down = own_block(
                i, g, heads, q_ref, g_ref, k_ref, v_ref, start_ref
            )
            query_rows.append(rows_i)
            grad_rows.append(grads_i)
            prev = dot(key_rows, rows_i, NT) * (SCALE * LOG2E)
            prev = masked(prev, start_ref[:, i * BLOCK : (i + 1) * BLOCK], -keys * BLOCK)
            dprev = dot(value_rows, grads_i, NT)
            top = jnp.maximum(
                jnp.max(own, axis=0, keepdims=True), jnp.max(prev, axis=0, keepdims=True)
            )
            own, prev = jnp.exp2(own - top), jnp.exp2(prev - top)
            total = jnp.sum(own, axis=0, keepdims=True) + jnp.sum(prev, axis=0, keepdims=True)
            dsum = jnp.sum(own * down, axis=0, keepdims=True) + jnp.sum(
                prev * dprev, axis=0, keepdims=True
            )
            stat_ref[i, 0:1, :] = top
            stat_ref[i, 1:2, :] = total
            stat_ref[i, 2:3, :] = dsum
            inverse = 1.0 / total
            prob = prev * inverse
            dscore = (prob * (dprev - dsum * inverse)).astype(jnp.bfloat16)
            probs.append(prob.astype(jnp.bfloat16))
            dscores.append(dscore)
        probs, dscores = (jnp.concatenate(x, axis=1) for x in (probs, dscores))
        query_rows, grad_rows = (jnp.concatenate(x, axis=0) for x in (query_rows, grad_rows))
        send_ref[seen, HEAD_WIDTH:] = dot(probs, grad_rows, NN).astype(jnp.bfloat16)
        send_ref[seen, :HEAD_WIDTH] = (dot(dscores, query_rows, NN) * SCALE).astype(jnp.bfloat16)
        dq = dot(key_rows, dscores, TN)
        for i in range(queries):
            dq_ref[i] = dq[:, i * heads * BLOCK : (i + 1) * heads * BLOCK]
        if keys < blocks:
            rest = slice(0, (blocks - keys) * BLOCK)
            send_ref[rest, :] = jnp.zeros(send_ref[rest, :].shape, jnp.bfloat16)

    for queries in range(1, blocks + 1):
        pl.when(after == queries)(functools.partial(crossing, blocks + 1 - queries, queries))

    @pl.when(after == 0)
    def _():
        send_ref[...] = jnp.zeros(send_ref.shape, jnp.bfloat16)


def own_kernel(kv_heads, *refs):
    first_ref, reach_ref, q_ref, g_ref, k_ref, v_ref, start_ref, stat_ref = refs[:8]
    per_head = [refs[8 + 2 * g : 10 + 2 * g] for g in range(kv_heads)]
    refs = refs[8 + 2 * kv_heads :]
    dq_hbm, keeps, (dq_ref, dk_ref, dv_ref, sums_ref, sems) = refs[0], refs[1 : 1 + kv_heads], refs[1 + kv_heads :]
    rows, width = q_ref.shape
    heads = width // k_ref.shape[1]
    blocks = rows // BLOCK
    reach = reach_ref[0]
    @pl.when(first_ref[0] == 0)
    def _():
        sums_ref[...] = stat_ref[...]

    for g in range(kv_heads):
        for i in range(blocks):

            @pl.when(i < reach)
            def _():
                sums_ref[g, i] = per_head[g][0][i]

            @pl.when((first_ref[0] > 0) & (i >= reach))
            def _():
                own_sums(sums_ref.at[g, i], i, g, heads, q_ref, g_ref, k_ref, v_ref, start_ref)

    copies = []
    for g in range(kv_heads):
        dqp_ref = per_head[g][1]
        for i in reversed(range(blocks)):
            seen = slice(0, (i + 1) * BLOCK)
            query_rows, grad_rows, own, down = own_block(
                i, g, heads, q_ref, g_ref, k_ref, v_ref, start_ref
            )
            top, total, dsum = (sums_ref[g, i, n : n + 1, :] for n in range(3))
            inverse = 1.0 / total
            own = jnp.exp2(own - top) * inverse
            down = (own * (down - dsum * inverse)).astype(jnp.bfloat16)
            dv = dot(own.astype(jnp.bfloat16), grad_rows, NN)
            dk = dot(down, query_rows, NN)
            if i == blocks - 1:
                dv_ref[...] = dv
                dk_ref[...] = dk
            else:
                dv_ref[seen, :] += dv
                dk_ref[seen, :] += dk
            dq = dot(k_ref[seen, column(g)], down, TN)
            dq = (dq + jnp.where(i < reach, dqp_ref[i], 0.0)) * SCALE
            place = (
                pl.ds(i * BLOCK, BLOCK),
                pl.ds(g * heads * HEAD_WIDTH, heads * HEAD_WIDTH),
            )
            for h in range(heads):
                dq_ref[place[0], pl.ds((g * heads + h) * HEAD_WIDTH, HEAD_WIDTH)] = jnp.transpose(
                    dq[:, h * BLOCK : (h + 1) * BLOCK]
                ).astype(jnp.bfloat16)
            copy = pltpu.make_async_copy(
                dq_ref.at[place], dq_hbm.at[place], sems.at[g * blocks + i]
            )
            copy.start()
            copies.append(copy)
        keeps[g][:, :HEAD_WIDTH] = dk_ref[...] * SCALE
        keeps[g][:, HEAD_WIDTH:] = dv_ref[...]
    for copy in copies:
        copy.wait()


def sum_kernel(keep_ref, back_ref, *refs):
    dk_ref, dv_ref = refs[-2:]
    total = keep_ref[...] + back_ref[...].astype(jnp.float32)
    dk_ref[...] = total[:, :HEAD_WIDTH].astype(jnp.bfloat16)
    dv_ref[...] = total[:, HEAD_WIDTH:].astype(jnp.bfloat16)


def body(queries, keys, values, output_gradient, doc_lengths):
    rows = queries.shape[0]
    kv_heads = keys.shape[1] // HEAD_WIDTH
    heads = queries.shape[1] // keys.shape[1]
    blocks = rows // BLOCK
    lanes = heads * BLOCK
    axes = ("seq", "head")
    prev_keys = rotated(keys, "seq", 1)
    prev_values = rotated(values, "seq", 1)
    row = lengths_row(doc_lengths, axes)
    known = []
    for group in round_groups():
        row = summed_round(row, axes, group)
        known.append(row)
    first = (lax.axis_index("seq") * rows).astype(jnp.int32).reshape(1)
    params = pltpu.CompilerParams(vmem_limit_bytes=24 * 1024 * 1024)
    shape = jax.ShapeDtypeStruct
    vmem = pl.BlockSpec(memory_space=pltpu.VMEM)
    smem = pl.BlockSpec(memory_space=pltpu.SMEM)
    hbm = pl.BlockSpec(memory_space=pltpu.HBM)
    pair = shape((rows, 2 * HEAD_WIDTH), jnp.bfloat16)
    per_head = [
        pair,
        shape((blocks, 8, lanes), jnp.float32),
        shape((blocks, HEAD_WIDTH, lanes), jnp.float32),
    ]
    arrays = (queries, output_gradient, keys, values)
    fetched = pl.pallas_call(
        functools.partial(fetch_kernel, len(arrays)),
        out_shape=[shape(a.shape, a.dtype) for a in arrays],
        in_specs=[hbm] * (1 + len(arrays)),
        out_specs=[vmem] * len(arrays),
        scratch_shapes=[pltpu.SemaphoreType.DMA((2 * len(arrays),))],
        compiler_params=params,
        name="fetch",
    )(known[1], *(pltpu.with_memory_space_constraint(a, pltpu.HBM) for a in arrays))
    first_stats = pl.pallas_call(
        first_kernel,
        out_shape=shape((kv_heads, blocks, 8, lanes), jnp.float32),
        in_specs=[smem] + [vmem] * 5,
        out_specs=vmem,
        scratch_shapes=[pltpu.VMEM((1, rows), jnp.int32)],
        compiler_params=params,
        name="first_sums",
    )(first, row, *fetched)
    send, stat, dq, reach, start = pl.pallas_call(
        functools.partial(prev_kernel, 0),
        out_shape=per_head
        + [shape((1,), jnp.int32), shape((1, rows), jnp.int32)],
        in_specs=[smem] + [vmem] * 8,
        out_specs=[vmem] * 3 + [smem, vmem],
        compiler_params=params,
        name="prev_grads",
    )(first, row, prev_keys, prev_values, *fetched, first_stats)
    sends, stats = [send], [stat, dq]
    for g in range(1, kv_heads):
        send, stat, dq = pl.pallas_call(
            functools.partial(prev_kernel, g),
            out_shape=per_head,
            in_specs=[smem] + [vmem] * 8,
            out_specs=[vmem] * 3,
            compiler_params=params,
            name="prev_grads",
        )(first, row, prev_keys, prev_values, *fetched, start)
        sends.append(send)
        stats += [stat, dq]
    backs = [rotated(send, "seq", -1) for send in sends]
    grad_queries, *keeps = pl.pallas_call(
        functools.partial(own_kernel, kv_heads),
        out_shape=[shape(queries.shape, jnp.bfloat16)]
        + [shape(pair.shape, jnp.float32)] * kv_heads,
        in_specs=[smem] * 2 + [vmem] * (6 + 2 * kv_heads),
        out_specs=[hbm] + [vmem] * kv_heads,
        scratch_shapes=[pltpu.VMEM(queries.shape, jnp.bfloat16)]
        + [pltpu.VMEM((rows, HEAD_WIDTH), jnp.float32)] * 2
        + [pltpu.VMEM((kv_heads, blocks, 8, lanes), jnp.float32)]
        + [pltpu.SemaphoreType.DMA((kv_heads * blocks,))],
        compiler_params=params,
        name="own_grads",
    )(first, reach, *fetched, start, first_stats, *stats)
    sums = []
    for g in range(kv_heads):
        whole = pl.BlockSpec(pair.shape, lambda n: (0, 0))
        sums = pl.pallas_call(
            sum_kernel,
            grid=(1,),
            out_shape=[shape(keys.shape, jnp.bfloat16)] * 2,
            in_specs=[whole] * 2 + [pl.BlockSpec(memory_space=pl.ANY)] * len(sums),
            out_specs=[pl.BlockSpec((rows, HEAD_WIDTH), lambda n, g=g: (0, g))] * 2,
            input_output_aliases={2: 0, 3: 1} if sums else {},
            compiler_params=params,
            name="sums",
        )(keeps[g], backs[g], *sums)
    key_gradient, value_gradient = sums
    return (grad_queries, key_gradient, value_gradient)


def solution(mesh):
    in_specs = (
        P("seq", "head"),
        P("seq", "head"),
        P("seq", "head"),
        P("seq", "head"),
        P(("seq", "head")),
    )
    out_specs = (P("seq", "head"), P("seq", "head"), P("seq", "head"))
    return jax.shard_map(body, mesh=mesh, in_specs=in_specs, out_specs=out_specs, check_vma=False)
```
